32 devices in a mesh: gx: 4 (over x, core), gy: 4 (over z), fsdp: 2 (over y).
Axes of the slice: x: 2, y: 2, z: 4, core: 2. Of those that a mesh axis runs over, the one named last changes fastest.
Arguments:
- tokens: bfloat16 [16384, 512], P(('gx', 'gy', 'fsdp')), may hold values from -6 to 6
- gain_one: float32 [512], replicated, may hold values from 0.1 to 1.9
- gain_two: float32 [512], replicated, may hold values from 0.1 to 1.9
- w_qkv: bfloat16 [1536, 512], P('fsdp'), may hold values from -1 to 1
- w_out: bfloat16 [512, 512], P('fsdp'), may hold values from -0.25 to 0.25
- w_in: bfloat16 [2048, 512], P('fsdp'), may hold values from -0.25 to 0.25
- w_down: bfloat16 [2048, 512], P('fsdp'), may hold values from -0.125 to 0.125
- send_x: int32 [4096], P(('gx', 'gy', 'fsdp')), may hold values from 0 to 511
- send_y: int32 [4096], P(('gx', 'gy', 'fsdp')), may hold values from 0 to 511
- context: int32 [128, 128], P(('gx', 'gy', 'fsdp')), may hold values from 0 to 767
- lengths: int32 [128], P(('gx', 'gy', 'fsdp')), may hold values from 1 to 128
Outputs:
- output: bfloat16 [16384, 512], P(('gx', 'gy', 'fsdp'))
The draws below stay inside these ranges and needn't reach their ends.
Inputs may be any that keep to these rules, and one draw needn't show every extreme that they name: `send_x`: row numbers inside the sending piece. `send_y`: row numbers inside the sending piece. `context`: row numbers inside the window's pool.
All inputs are finite; a program needn't handle non-finite values.
Results may differ from the reference program's by a relative error of at most 0.0094.
Values may be sent and summed in bfloat16 or wider, within the bound.
No kernel may reach another device: no remote copies, remote signals or barrier semaphores. Data moves between devices by JAX's collectives and lax.ppermute only.
A program may use at most 64 MiB of HBM per device.

```python
import jax
import jax.numpy as jnp
from jax import lax

D = 512
HEADS = 16
FF = 2048
WIN = 128
CTX = 128
HALO = 128
TOK_DEV = 512
TOKENS = 16384
WINDOWS = 128
SENDS = 4096
N_GX = 4
N_GY = 4
N_FSDP = 2


def draw_w_qkv(key, part):
    key = jax.random.fold_in(key, 11)
    base = jax.random.normal(key, (3 * D, D), jnp.float32) * D ** (-0.5)
    return jnp.clip(base, -1.0, 1.0).astype(jnp.bfloat16)


def set_ends(drawn, rng, low, high):
    longest = drawn.shape.index(max(drawn.shape))
    spots = []
    for shift in (0, 1):
        where = [jax.random.randint(jax.random.fold_in(rng, axis), (), 0, length) for axis, length in enumerate(drawn.shape)]
        where[longest] = (where[longest] + shift) % drawn.shape[longest]
        spots.append(tuple(where))
    return drawn.at[spots[0]].set(low).at[spots[1]].set(high)


def level_of(key, extent, shards, low, top_value):
    def one(dim, parts):
        heights = jax.random.uniform(jax.random.fold_in(jax.random.fold_in(key, 6), dim), (parts,), jnp.float32, low / len(shards), top_value / len(shards))
        return jnp.repeat(jnp.exp(heights), extent[dim] // parts).reshape((-1,) + (1,) * (len(extent) - dim - 1))

    factor_of = one(*shards[0])
    for cut in shards[1:]:
        factor_of = factor_of * one(*cut)
    return factor_of


def gaussian(stream_key, dims, scale, bound, pieces=(), held_as=jnp.bfloat16):
    level = level_of(stream_key, dims, pieces, -0.22, 0.18) if pieces else 1.0
    entries = jax.random.normal(stream_key, dims, jnp.float32) * scale * level
    return jnp.minimum(jnp.maximum(entries, -bound), bound).astype(held_as)


def setup_inputs(seed: int = 0) -> dict:
    arg_keys = jax.random.split(jax.random.key(seed), 12)
    return {
        "tokens": gaussian(arg_keys[0], (TOKENS, D), 1.0, 6.0, ((0, 32),)),
        "gain_one": jnp.clip(1.0 + 0.18 * jax.random.normal(arg_keys[1], (D,), jnp.float32), 0.1, 1.9),
        "gain_two": jnp.clip(1.0 + 0.18 * jax.random.normal(arg_keys[2], (D,), jnp.float32), 0.1, 1.9),
        "w_qkv": draw_w_qkv(jax.random.fold_in(arg_keys[11], 71), 0),
        "w_out": gaussian(arg_keys[4], (D, D), D ** -0.5, 0.25, ((0, 2),)),
        "w_in": gaussian(arg_keys[5], (FF, D), D ** -0.5, 0.25, ((0, 2),)),
        "w_down": gaussian(arg_keys[6], (FF, D), FF ** -0.5, 0.125, ((0, 2),)),
        "send_x": set_ends(jax.random.randint(arg_keys[7], (SENDS,), 0, TOK_DEV), jax.random.fold_in(arg_keys[7], 1), 0, TOK_DEV - 1).astype(jnp.int32),
        "send_y": set_ends(jax.random.randint(arg_keys[8], (SENDS,), 0, TOK_DEV), jax.random.fold_in(arg_keys[8], 1), 0, TOK_DEV - 1).astype(jnp.int32),
        "context": set_ends(jax.random.randint(arg_keys[9], (WINDOWS, CTX), 0, TOK_DEV + 2 * HALO), jax.random.fold_in(arg_keys[9], 1), 0, (TOK_DEV + 2 * HALO) - 1).astype(jnp.int32),
        "lengths": set_ends(jax.random.randint(arg_keys[10], (WINDOWS,), 1, WIN + 1), jax.random.fold_in(arg_keys[10], 1), 1, WIN).astype(jnp.int32),
    }


EPSILON = 1e-05

def layer_norm(values, gain):
    values = values.astype(jnp.float32)
    center = values - lax.optimization_barrier(jnp.mean(values, axis=-1, keepdims=True))
    spread = lax.optimization_barrier(jnp.mean(center * center, axis=-1, keepdims=True))
    return (center * lax.rsqrt(spread + EPSILON) * gain).astype(jnp.bfloat16)

def attend(projected, pool, chosen, window_lengths):
    width = projected.shape[1] // 3
    count = projected.shape[0] // WIN
    head_size = width // HEADS
    queries = projected[:, :width].reshape(count, WIN, HEADS, head_size).astype(jnp.float32)
    gathered = jnp.take(pool, chosen, axis=0)
    own_pairs = projected[:, width:].reshape(count, WIN, 2 * width)
    pairs = jnp.concatenate([own_pairs, gathered], axis=1).astype(jnp.float32)
    keys = pairs[..., :width].reshape(count, WIN + CTX, HEADS, head_size)
    values = pairs[..., width:].reshape(count, WIN + CTX, HEADS, head_size)
    keep = jnp.concatenate([jnp.arange(WIN)[None, :] < window_lengths[:, None], jnp.ones((count, CTX), dtype=bool)], axis=1)
    scores = jnp.einsum('wqhe,wkhe->whqk', queries, keys) * head_size ** (-0.5)
    scores = jnp.where(keep[:, None, None, :], scores, -1e+30)
    largest = lax.optimization_barrier(jnp.max(scores, axis=-1, keepdims=True))
    expo = jnp.exp(scores - largest)
    total = lax.optimization_barrier(jnp.sum(expo, axis=-1, keepdims=True))
    probs = (expo / total).astype(jnp.bfloat16)
    mixed = jnp.einsum('whqk,wkhe->wqhe', probs.astype(jnp.float32), values)
    return mixed.reshape(count * WIN, width).astype(jnp.bfloat16)

def reference(tokens, gain_one, gain_two, w_qkv, w_out, w_in, w_down, send_x, send_y, context, lengths):
    devices = N_GX * N_GY * N_FSDP
    width = tokens.shape[1]
    count = TOK_DEV // WIN

    def neighbour(source, present, sends):
        source = jnp.where(present, source, 0).astype(jnp.int32)
        block = lax.dynamic_slice_in_dim(tokens, source * TOK_DEV, TOK_DEV, 0)
        listed = lax.dynamic_slice_in_dim(sends, source * HALO, HALO, 0)
        normed = layer_norm(jnp.take(block, listed, axis=0), gain_one)
        pairs = jnp.dot(normed, w_qkv[width:].T, preferred_element_type=jnp.float32).astype(jnp.bfloat16)
        return jnp.where(present, pairs, jnp.zeros_like(pairs))

    def one_piece(device):
        block = lax.dynamic_slice_in_dim(tokens, (device * TOK_DEV).astype(jnp.int32), TOK_DEV, 0)
        normed = layer_norm(block, gain_one)
        projected = jnp.dot(normed, w_qkv.T, preferred_element_type=jnp.float32).astype(jnp.bfloat16)
        halo_x = neighbour(device - N_GY * N_FSDP, device >= N_GY * N_FSDP, send_x)
        halo_y = neighbour(device - N_FSDP, device // N_FSDP % N_GY > 0, send_y)
        pool = jnp.concatenate([projected[:, width:], halo_x, halo_y], axis=0)
        chosen = lax.dynamic_slice_in_dim(context, (device * count).astype(jnp.int32), count, 0)
        window_lengths = lax.dynamic_slice_in_dim(lengths, (device * count).astype(jnp.int32), count, 0)
        mixed = attend(projected, pool, chosen, window_lengths)
        middle = block.astype(jnp.float32) + jnp.dot(mixed, w_out.T, preferred_element_type=jnp.float32)
        second = layer_norm(middle, gain_two)
        hidden = jax.nn.gelu(jnp.dot(second, w_in.T, preferred_element_type=jnp.float32)).astype(jnp.bfloat16)
        return (middle + jnp.dot(hidden, w_down, preferred_element_type=jnp.float32)).astype(jnp.bfloat16)
    results = lax.map(one_piece, jnp.arange(devices, dtype=jnp.int32))
    return results.reshape(devices * TOK_DEV, width)
```

```python
import jax
import jax.numpy as jnp
from jax import lax
from jax.experimental import pallas as pl
from jax.experimental.pallas import tpu as pltpu
from jax.sharding import PartitionSpec as P

HEADS = 16
WIN = 128
CTX = 128
LANES = 128
EPSILON = 1e-05
LOG2E = 1.4426950408889634

VMEM = pl.BlockSpec(memory_space=pltpu.VMEM)
SMEM = pl.BlockSpec(memory_space=pltpu.SMEM)
ANY = pl.BlockSpec(memory_space=pl.ANY)
PARAMS = pltpu.CompilerParams(vmem_limit_bytes=40 * 1024 * 1024)


def shifted(value, axis, steps):
    count = lax.axis_size(axis)
    initial, last = (max(0, -steps), min(count, count - steps))
    return lax.ppermute(value, axis, [(source, source + steps) for source in range(initial, last)])


def dot_nt(left, right):
    return lax.dot_general(left, right, (((1,), (1,)), ((), ())), preferred_element_type=jnp.float32)


def dot_nn(left, right):
    return jnp.dot(left, right, preferred_element_type=jnp.float32)


def layer_norm(values, gain):
    values = values.astype(jnp.float32)
    center = values - jnp.mean(values, axis=-1, keepdims=True)
    spread = jnp.mean(center * center, axis=-1, keepdims=True)
    return (center * lax.rsqrt(spread + EPSILON) * gain).astype(jnp.bfloat16)


def pick_rows(indices, count):
    column = jnp.broadcast_to(indices.astype(jnp.float32), (LANES, LANES)).T
    lane = lax.broadcasted_iota(jnp.int32, (LANES, LANES), 1).astype(jnp.float32)
    blocks = [
        jnp.where(column == lane + float(first), 1.0, 0.0).astype(jnp.bfloat16)
        for first in range(0, count, LANES)
    ]
    return jnp.concatenate(blocks, axis=1)


def norm_kernel(tokens, gain, send_x, send_y, out_x, out_y, normed):
    rows = tokens.shape[0]
    block = tokens[...]
    out_x[...] = dot_nn(pick_rows(send_x[...], rows), block).astype(jnp.bfloat16)
    out_y[...] = dot_nn(pick_rows(send_y[...], rows), block).astype(jnp.bfloat16)
    normed[...] = layer_norm(block, gain[...])


def context_kernel(normed, halo_x, halo_y, gain, context, chosen):
    pool = jnp.concatenate(
        [normed[...], layer_norm(halo_x[...], gain[...]), layer_norm(halo_y[...], gain[...])], axis=0
    )
    for window in range(context.shape[0]):
        picked = dot_nn(pick_rows(context[pl.ds(window, 1), :], pool.shape[0]), pool)
        chosen[pl.ds(window * CTX, CTX), :] = picked.astype(jnp.bfloat16)


def load_pieces(places, pieces, target, sems):
    copies = []
    for number, piece in enumerate(pieces):
        rows = piece.shape[0]
        start = pl.multiple_of(places[number], 16)
        copy = pltpu.make_async_copy(piece, target.at[pl.ds(start, rows), :], sems.at[number])
        copy.start()
        copies.append(copy)
    return copies


def attention_kernel(count, *refs):
    lengths, qkv_places, out_places, normed, chosen, tokens, gain = refs[:7]
    qkv_pieces = refs[7 : 7 + count]
    out_pieces = refs[7 + count : 7 + 2 * count]
    middle, second, w_qkv, w_out, mixed, sems = refs[7 + 2 * count :]
    width = tokens.shape[1]
    head_size = width // HEADS
    group = LANES // head_size
    qkv_copies = load_pieces(qkv_places, qkv_pieces, w_qkv, sems.at[0])
    out_copies = load_pieces(out_places, out_pieces, w_out, sems.at[1])
    for copy in qkv_copies:
        copy.wait()
    own, ctx = normed[...], chosen[...]
    w_q, w_k, w_v = (w_qkv[pl.ds(part * width, width), :] for part in range(3))
    queries = dot_nt(w_q, own).astype(jnp.bfloat16)
    own_keys = dot_nt(own, w_k).astype(jnp.bfloat16)
    ctx_keys = dot_nt(ctx, w_k).astype(jnp.bfloat16)
    own_values = dot_nt(w_v, own).astype(jnp.bfloat16)
    ctx_values = dot_nt(w_v, ctx).astype(jnp.bfloat16)
    scale = head_size ** (-0.5) * LOG2E
    for window in range(tokens.shape[0] // WIN):
        low, high = window * WIN, (window + 1) * WIN
        length = lengths[window]
        row = lax.broadcasted_iota(jnp.int32, (WIN, 1), 0)
        keys = jnp.concatenate(
            [
                jnp.where(row < length, own_keys[low:high], ctx_keys[low : low + 1]),
                ctx_keys[low:high],
            ],
            axis=0,
        )
        slot = lax.broadcasted_iota(jnp.int32, (1, WIN), 1)
        values = jnp.concatenate(
            [
                jnp.where(slot < length, own_values[:, low:high], jnp.zeros((), jnp.bfloat16)),
                ctx_values[:, low:high],
            ],
            axis=1,
        )
        slots = lax.broadcasted_iota(jnp.int32, (16, WIN + CTX), 1)
        ones = jnp.where((slots < length) | (slots >= WIN), 1.0, 0.0).astype(jnp.bfloat16)
        for first in range(0, width, LANES):
            group_queries = queries[first : first + LANES, low:high]
            parts = []
            for head in range(group):
                pad = [jnp.zeros((head_size, WIN), jnp.bfloat16)] * group
                pad[head] = group_queries[head * head_size : (head + 1) * head_size]
                parts.append(jnp.concatenate(pad, axis=0))
            scores = dot_nn(keys[:, first : first + LANES], jnp.concatenate(parts, axis=1))
            largest = jnp.max(scores, axis=0, keepdims=True)
            probs = jnp.exp2((scores - largest) * scale).astype(jnp.bfloat16)
            outs = []
            for head in range(0, group, 2):
                top = first + head * head_size
                weights = jnp.concatenate([values[top : top + 2 * head_size], ones], axis=0)
                sums = dot_nn(weights, probs[:, head * WIN : (head + 2) * WIN])
                for part in range(2):
                    block = sums[:, part * WIN : (part + 1) * WIN]
                    outs.append(
                        block[part * head_size : (part + 1) * head_size]
                        * (1.0 / block[2 * head_size : 2 * head_size + 1])
                    )
            mixed[low:high, first : first + LANES] = jnp.concatenate(outs, axis=0).T.astype(jnp.bfloat16)
    for copy in out_copies:
        copy.wait()
    total = tokens[...].astype(jnp.float32) + dot_nt(mixed[...], w_out[...])
    middle[...] = total
    second[...] = layer_norm(total, gain[...])


def feed_kernel(count, middle, second, *refs):
    output = refs[2 * count]
    total = middle[...]
    for number in range(count):
        hidden = jax.nn.gelu(dot_nt(second[...], refs[number][...])).astype(jnp.bfloat16)
        total = total + dot_nn(hidden, refs[count + number][...])
    output[...] = total.astype(output.dtype)


def gather_pieces(weights):
    ranks, cores = lax.axis_size("fsdp"), lax.axis_size("gx")
    if ranks != 2 or cores % 2:
        return [
            ([lax.all_gather(weight, "fsdp", axis=0, tiled=True)], jnp.zeros((1,), jnp.int32))
            for weight in weights
        ]
    rank = lax.axis_index("fsdp")
    core = lax.axis_index("gx") % 2
    swap = [(core_index, core_index ^ 1) for core_index in range(cores)]
    results = []
    for weight in weights:
        rows = weight.shape[0]
        half = rows // 2
        mine = lax.dynamic_slice_in_dim(weight, core * half, half, 0)
        theirs = lax.ppermute(mine, "fsdp", [(0, 1), (1, 0)])
        rest = lax.ppermute(theirs, "gx", swap)
        base = (1 - rank) * rows
        places = jnp.stack([rank * rows, base + core * half, base + (1 - core) * half])
        results.append(([weight, theirs, rest], places.astype(jnp.int32)))
    return results


def body(tokens, gain_one, gain_two, w_qkv, w_out, w_in, w_down, send_x, send_y, context, lengths):
    rows, width = tokens.shape
    halo = send_x.shape[0]
    gain_one, gain_two = gain_one[None, :], gain_two[None, :]
    gathered = gather_pieces([w_qkv, w_out, w_in, w_down])
    (qkv, qkv_places), (out, out_places), (into, _), (down, _) = gathered
    half = jax.ShapeDtypeStruct((rows, width), jnp.bfloat16)
    full = jax.ShapeDtypeStruct((rows, width), jnp.float32)
    edge = jax.ShapeDtypeStruct((halo, width), jnp.bfloat16)
    out_x, out_y, normed = pl.pallas_call(
        norm_kernel, out_shape=(edge, edge, half), in_specs=[VMEM] * 4, out_specs=(VMEM,) * 3,
        compiler_params=PARAMS, name="norm",
    )(tokens, gain_one, send_x[None, :], send_y[None, :])
    halo_x = shifted(out_x, "gx", 1)
    halo_y = shifted(out_y, "gy", 1)
    chosen = pl.pallas_call(
        context_kernel, out_shape=half, in_specs=[VMEM] * 5, out_specs=VMEM,
        compiler_params=PARAMS, name="context",
    )(normed, halo_x, halo_y, gain_one, context)
    count = len(qkv)
    middle, second = pl.pallas_call(
        lambda *refs: attention_kernel(count, *refs),
        out_shape=(full, half),
        in_specs=[SMEM] * 3 + [VMEM] * 4 + [ANY] * (2 * count),
        out_specs=(VMEM, VMEM),
        scratch_shapes=[
            pltpu.VMEM((3 * width, width), jnp.bfloat16),
            pltpu.VMEM((width, width), jnp.bfloat16),
            pltpu.VMEM((rows, width), jnp.bfloat16),
            pltpu.SemaphoreType.DMA((2, count)),
        ],
        compiler_params=PARAMS, name="attention",
    )(lengths, qkv_places, out_places, normed, chosen, tokens, gain_two, *qkv, *out)

    def feed(total, first, last, dtype):
        number = last - first
        return pl.pallas_call(
            lambda *refs: feed_kernel(number, *refs),
            out_shape=jax.ShapeDtypeStruct((rows, width), dtype),
            in_specs=[VMEM] * (2 + 2 * number), out_specs=VMEM,
            compiler_params=PARAMS, name="feed",
        )(total, second, *into[first:last], *down[first:last])

    if count == 1:
        return feed(middle, 0, 1, jnp.bfloat16)
    partial = feed(middle, 0, 1, jnp.float32)
    return feed(partial, 1, count, jnp.bfloat16)


def solution(mesh):
    in_specs = (
        P(("gx", "gy", "fsdp"), None),
        P(),
        P(),
        P("fsdp", None),
        P("fsdp", None),
        P("fsdp", None),
        P("fsdp", None),
        P(("gx", "gy", "fsdp")),
        P(("gx", "gy", "fsdp")),
        P(("gx", "gy", "fsdp"), None),
        P(("gx", "gy", "fsdp")),
    )
    out_specs = P(("gx", "gy", "fsdp"), None)
    return jax.shard_map(body, mesh=mesh, in_specs=in_specs, out_specs=out_specs, check_vma=False)
```

```python
import typing

import jax
import jax.numpy as jnp
from jax import lax
from jax.experimental import pallas as pl
from jax.experimental.pallas import tpu as pltpu
from jax.sharding import PartitionSpec as P

HEADS = 16
WIN = 128
CTX = 128
LANES = 128
EPSILON = 1e-05
LOG2E = 1.4426950408889634

VMEM = pl.BlockSpec(memory_space=pltpu.VMEM)
SMEM = pl.BlockSpec(memory_space=pltpu.SMEM)
HBM = pl.BlockSpec(memory_space=pltpu.HBM)
PARAMS = pltpu.CompilerParams(vmem_limit_bytes=16 * 1024 * 1024)


def ring(value, axis):
    count = lax.axis_size(axis)
    return lax.ppermute(value, axis, [(source, (source + 1) % count) for source in range(count)])


def swap(value, axis, bit):
    count = lax.axis_size(axis)
    return lax.ppermute(value, axis, [(source, source ^ bit) for source in range(count)])


def dot_nt(left, right):
    return lax.dot_general(left, right, (((1,), (1,)), ((), ())), preferred_element_type=jnp.float32)


def dot_nn(left, right):
    return jnp.dot(left, right, preferred_element_type=jnp.float32)


def layer_norm(values, gain):
    values = values.astype(jnp.float32)
    center = values - jnp.mean(values, axis=-1, keepdims=True)
    spread = jnp.mean(center * center, axis=-1, keepdims=True)
    return (center * lax.rsqrt(spread + EPSILON) * gain).astype(jnp.bfloat16)


def pick_rows(indices, count):
    column = jnp.broadcast_to(indices.astype(jnp.float32), (LANES, LANES)).T
    lane = lax.broadcasted_iota(jnp.int32, (LANES, LANES), 1).astype(jnp.float32)
    blocks = [
        jnp.where(column == lane + float(first), 1.0, 0.0).astype(jnp.bfloat16)
        for first in range(0, count, LANES)
    ]
    return jnp.concatenate(blocks, axis=1)


def norm_kernel(tokens, gain, send_x, send_y, out_x, out_y, normed):
    rows = tokens.shape[0]
    block = tokens[...]
    out_x[...] = dot_nn(pick_rows(send_x[...], rows), block).astype(jnp.bfloat16)
    out_y[...] = dot_nn(pick_rows(send_y[...], rows), block).astype(jnp.bfloat16)
    normed[...] = layer_norm(block, gain[...])


def present(halo, axis):
    return jnp.where(lax.axis_index(axis) > 0, halo[...].astype(jnp.float32), 0.0)


def context_kernel(lengths, normed, halo_x, halo_y, gain, context, chosen, filled):
    parts = [layer_norm(present(halo_x, "gx"), gain[...]), layer_norm(present(halo_y, "gy"), gain[...])]
    pool = jnp.concatenate([normed[...]] + parts, axis=0)
    for window in range(context.shape[0]):
        picked = dot_nn(pick_rows(context[pl.ds(window, 1), :], pool.shape[0]), pool)
        chosen[pl.ds(window * CTX, CTX), :] = picked.astype(jnp.bfloat16)
        filled[pl.ds(window, 1), :] = jnp.full((1, LANES), lengths[window], jnp.int32)


class Share(typing.NamedTuple):
    base: int
    axis: str
    stride: int
    rows: int

    def start(self, flip):
        core = lax.axis_index("gx") % 2
        index = {
            "core": lambda: core,
            "gx": lambda: lax.axis_index("gx"),
            "gy": lambda: (lax.axis_index("gy") % 2) * 2 + core,
        }[self.axis]()
        return self.base + (index ^ flip) * self.stride


def slice_kernel(shares, *refs):
    count = len(shares)
    shards, parts, sems = refs[:count], refs[count : 2 * count], refs[2 * count]
    copies = []
    for number, share in enumerate(shares):
        start = pl.multiple_of(share.start(0), 32)
        copies.append(
            pltpu.make_async_copy(shards[number].at[pl.ds(start, share.rows), :], parts[number], sems.at[number])
        )
    for copy in copies:
        copy.start()
    for copy in copies:
        copy.wait()


def prepare_kernel(shares, *refs):
    count = len(shares)
    sources, shards, refs = refs[:4], refs[4 : 4 + count], refs[4 + count :]
    (held, out_x, out_y, normed), parts, scratch, sems = refs[:4], refs[4 : 4 + count], refs[4 + count : -1], refs[-1]
    copies = []
    for source, target in zip(sources, (held, *scratch)):
        copies.append(pltpu.make_async_copy(source, target, sems.at[len(copies)]))
    for number, share in enumerate(shares):
        start = pl.multiple_of(share.start(0), 32)
        copies.append(
            pltpu.make_async_copy(shards[number].at[pl.ds(start, share.rows), :], parts[number], sems.at[len(copies)])
        )
    for copy in copies:
        copy.start()
    for copy in copies[:4]:
        copy.wait()
    norm_kernel(held, *scratch, out_x, out_y, normed)
    for copy in copies[4:]:
        copy.wait()


def assemble(whole, own, pieces):
    if not pieces:
        whole[...] = own[...]
        return
    rank = lax.axis_index("fsdp")
    rows = own.shape[0]
    whole[pl.ds(pl.multiple_of(rank * rows, rows), rows), :] = own[...]
    for share, flip, value in pieces:
        start = pl.multiple_of((1 - rank) * rows + share.start(flip), 32)
        whole[pl.ds(start, share.rows), :] = value[...]


def project_kernel(plan, normed, chosen, shard, *refs):
    pieces = refs[: len(plan)]
    queries, own_keys, ctx_keys, own_values, ctx_values, w_qkv = refs[len(plan) :]
    width = normed.shape[1]
    assemble(w_qkv, shard, [(*where, piece) for where, piece in zip(plan, pieces)])
    own, ctx = normed[...], chosen[...]
    w_q, w_k, w_v = (w_qkv[pl.ds(part * width, width), :] for part in range(3))
    queries[...] = dot_nt(w_q, own).astype(jnp.bfloat16)
    own_keys[...] = dot_nt(own, w_k).astype(jnp.bfloat16)
    ctx_keys[...] = dot_nt(ctx, w_k).astype(jnp.bfloat16)
    own_values[...] = dot_nt(w_v, own).astype(jnp.bfloat16)
    ctx_values[...] = dot_nt(w_v, ctx).astype(jnp.bfloat16)


def attend_kernel(windows, filled, queries, own_keys, ctx_keys, own_values, ctx_values, mixed):
    width = queries.shape[0]
    head_size = width // HEADS
    group = LANES // head_size
    scale = head_size ** (-0.5) * LOG2E
    for window in windows:
        low, high = window * WIN, (window + 1) * WIN
        base = low - windows[0] * WIN
        length = filled[window : window + 1, :]
        row_full = lax.broadcasted_iota(jnp.int32, (WIN, LANES), 0) < length
        row_full = jnp.concatenate([row_full] * (width // LANES), axis=1)
        keys = jnp.concatenate(
            [
                jnp.where(row_full, own_keys[low:high, :], ctx_keys[low : low + 1, :]),
                ctx_keys[low:high, :],
            ],
            axis=0,
        )
        slot_full = lax.broadcasted_iota(jnp.int32, (1, WIN), 1) < length
        values = jnp.concatenate(
            [
                jnp.where(slot_full, own_values[:, low:high], jnp.zeros((), jnp.bfloat16)),
                ctx_values[:, low:high],
            ],
            axis=1,
        )
        slots = lax.broadcasted_iota(jnp.int32, (16, WIN), 1) < length
        ones = jnp.concatenate([jnp.where(slots, 1.0, 0.0), jnp.ones((16, CTX), jnp.float32)], axis=1).astype(jnp.bfloat16)
        for first in range(0, width, LANES):
            group_queries = queries[first : first + LANES, low:high]
            parts = []
            for head in range(group):
                pad = [jnp.zeros((head_size, WIN), jnp.bfloat16)] * group
                pad[head] = group_queries[head * head_size : (head + 1) * head_size]
                parts.append(jnp.concatenate(pad, axis=0))
            scores = dot_nn(keys[:, first : first + LANES], jnp.concatenate(parts, axis=1))
            largest = jnp.max(scores, axis=0, keepdims=True)
            probs = jnp.exp2((scores - largest) * scale).astype(jnp.bfloat16)
            outs = []
            for head in range(0, group, 2):
                top = first + head * head_size
                weights = jnp.concatenate([values[top : top + 2 * head_size], ones], axis=0)
                sums = dot_nn(weights, probs[:, head * WIN : (head + 2) * WIN])
                for part in range(2):
                    block = sums[:, part * WIN : (part + 1) * WIN]
                    outs.append(
                        block[part * head_size : (part + 1) * head_size]
                        * (1.0 / block[2 * head_size : 2 * head_size + 1])
                    )
            mixed[base : base + WIN, first : first + LANES] = (
                jnp.concatenate(outs, axis=0).T.astype(jnp.bfloat16)
            )


def finish_kernel(parts, plan, tokens, gain, shard, *refs):
    mixed, pieces = refs[:parts], refs[parts : parts + len(plan)]
    middle, second, w_out = refs[parts + len(plan) :]
    assemble(w_out, shard, [(*where, piece) for where, piece in zip(plan, pieces)])
    low = 0
    for block in mixed:
        rows = slice(low, low + block.shape[0])
        total = tokens[rows, :].astype(jnp.float32) + dot_nt(block[...], w_out[...])
        middle[rows, :] = total
        second[rows, :] = layer_norm(total, gain[...])
        low += block.shape[0]


def columns_of(plan, number, piece):
    if not plan:
        return slice(None)
    share, flip = plan[number]
    return pl.ds(pl.multiple_of(share.start(flip), LANES), share.rows)


def hidden_kernel(plan, second, *refs):
    hidden = refs[-1]
    for number, piece in enumerate(refs[:-1]):
        units = jax.nn.gelu(dot_nt(second[...], piece[...])).astype(jnp.bfloat16)
        hidden[:, columns_of(plan, number, piece)] = units


def down_kernel(plan, start, hidden, *refs):
    output = refs[-1]
    total = start[...]
    for number, piece in enumerate(refs[:-1]):
        total = total + dot_nn(hidden[:, columns_of(plan, number, piece)], piece[...])
    output[...] = total.astype(output.dtype)


def last_kernel(plan, start, hidden, *refs):
    pieces, output, held, sems = refs[: len(plan)], refs[-3], refs[-2], refs[-1]
    blocks = start.shape[0] // WIN
    copies = []
    for block in range(blocks):
        rows = slice(block * WIN, (block + 1) * WIN)
        total = start[rows, :]
        for number, piece in enumerate(pieces):
            total = total + dot_nn(hidden[rows, columns_of(plan, number, piece)], piece[...])
        held[rows, :] = total.astype(output.dtype)
        copies.append(pltpu.make_async_copy(held.at[rows, :], output.at[rows, :], sems.at[block]))
        copies[-1].start()
    for copy in copies:
        copy.wait()


COSTS = {"norm": 1, "slices": 1, "prepare": 1, "context": 1, "project": 1, "attend": 1, "finish": 1, "hidden": 1, "down": 1}


def call(kernel, outs, operands, name, scratch=(), specs=None, result=VMEM):
    specs = specs or [VMEM] * len(operands)
    placed = [
        pltpu.with_memory_space_constraint(operand, pltpu.HBM) if spec is HBM else operand
        for operand, spec in zip(operands, specs)
    ]
    if result is VMEM:
        outs = [pltpu.VMEM(out.shape, out.dtype) for out in outs]
    return pl.pallas_call(
        kernel,
        out_shape=tuple(outs),
        in_specs=specs,
        out_specs=tuple(result or VMEM for _ in outs),
        scratch_shapes=list(scratch),
        compiler_params=PARAMS,
        name=name,
        cost_estimate=pl.CostEstimate(flops=COSTS[name] * 10**7, bytes_accessed=0, transcendentals=0),
    )(*placed)


def struct(rows, width, dtype=jnp.bfloat16):
    return jax.ShapeDtypeStruct((rows, width), dtype)


def body(tokens, gain_one, gain_two, w_qkv, w_out, w_in, w_down, send_x, send_y, context, lengths):
    rows, width = tokens.shape
    halo = send_x.shape[0]
    gain_one, gain_two = gain_one[None, :], gain_two[None, :]
    send_x, send_y = send_x[None, :], send_y[None, :]
    after = lax.optimization_barrier
    paired = lax.axis_size("fsdp") == 2 and lax.axis_size("gx") == 4 and lax.axis_size("gy") % 2 == 0
    edges = [struct(halo, width), struct(halo, width), struct(rows, width)]

    if not paired:
        qkv, out, into, down = (
            lax.all_gather(weight, "fsdp", axis=0, tiled=True) for weight in (w_qkv, w_out, w_in, w_down)
        )
        out_x, out_y, normed = call(norm_kernel, edges, (tokens, gain_one, send_x, send_y), "norm")
    else:
        qkv, out, into, down = w_qkv, w_out, w_in, w_down
        size = qkv.shape[0] // 4
        share_qkv = [Share(chunk * size, "core", 2 * size, size) for chunk in range(2)]
        share_out = Share(0, "core", out.shape[0] // 2, out.shape[0] // 2)
        share_in = Share(0, "gy", into.shape[0] // 4, into.shape[0] // 4)
        size = down.shape[0] // 8
        share_early = Share(0, "gx", size, size)
        share_late = Share(4 * size, "core", 2 * size, 2 * size)
        tokens, out_x, out_y, normed, *parts_qkv = call(
            lambda *refs: prepare_kernel(share_qkv, *refs),
            [struct(rows, width)] + edges + [struct(share.rows, width) for share in share_qkv],
            (tokens, gain_one, send_x, send_y, qkv, qkv), "prepare",
            [
                pltpu.VMEM(gain_one.shape, gain_one.dtype), pltpu.VMEM(send_x.shape, send_x.dtype),
                pltpu.VMEM(send_y.shape, send_y.dtype), pltpu.SemaphoreType.DMA((6,)),
            ],
            [HBM] * 6,
        )
        y_qkv = [swap(part, "fsdp", 1) for part in parts_qkv]
        shares = [share_in, share_out, share_early, share_late]
        later, normed = after(((w_in, w_out, w_down), normed))
        parts = call(
            lambda *refs: slice_kernel(shares, *refs), [struct(share.rows, width) for share in shares],
            (later[0], later[1], later[2], later[2]), "slices", [pltpu.SemaphoreType.DMA((4,))], [HBM] * 4,
        )
        y_in, y_out, y_early, y_late = (swap(part, "fsdp", 1) for part in parts)

    def crossed(share, near, flip=0):
        return [(share, flip, near), (share, flip + 1, swap(near, "gx", 1))]

    def arrays(pieces):
        return [piece[2] for piece in pieces]

    def plan(pieces):
        return [piece[:2] for piece in pieces]

    halo_x = ring(out_x, "gx")
    halo_y = ring(out_y, "gy")
    if paired:
        y_qkv[1], halo_x, halo_y = after((y_qkv[1], halo_x, halo_y))
    chosen, filled = call(
        context_kernel, [struct(rows, width), struct(*context.shape, jnp.int32)],
        (lengths, normed, halo_x, halo_y, gain_one, context), "context", specs=[SMEM] + [VMEM] * 5,
    )
    pieces = []
    if paired:
        for share, piece in zip(share_qkv, y_qkv):
            pieces += crossed(share, piece)
    projected = call(
        lambda *refs, plan=plan(pieces): project_kernel(plan, *refs), [struct(rows, width)] * 5,
        (normed, chosen, qkv, *arrays(pieces)), "project", [pltpu.VMEM((3 * width, width), jnp.bfloat16)],
    )

    def attend(windows):
        return call(
            lambda *refs: attend_kernel(windows, *refs), [struct(len(windows) * WIN, width)],
            (filled, *projected), "attend",
        )

    windows = list(range(rows // WIN))
    half = len(windows) // 2
    mixed = attend(windows[:half])
    pieces_out, pieces_in, pieces_down, pieces_last = [], [], [], []
    if paired:
        y_in, mixed = after((y_in, mixed))
        z_in = swap(y_in, "gy", 1)
        projected, y_in = after((projected, y_in))
    mixed += attend(windows[half:])
    if paired:
        y_out, y_early, mixed = after((y_out, y_early, mixed))
        pieces_out = crossed(share_out, y_out)
        x_early = swap(y_early, "gx", 2)
    middle, second = call(
        lambda *refs: finish_kernel(len(mixed), plan(pieces_out), *refs),
        [struct(rows, width, jnp.float32), struct(rows, width)], (tokens, gain_two, out, *mixed, *arrays(pieces_out)),
        "finish", [pltpu.VMEM((width, width), jnp.bfloat16)],
    )

    def expand(own, pieces):
        (hidden,) = call(
            lambda *refs: hidden_kernel(plan(pieces), *refs), [struct(rows, into.shape[0])],
            (second, *(arrays(pieces) or [own])), "hidden",
        )
        return hidden

    if not paired:
        return call(
            lambda *refs: down_kernel([], *refs), [struct(rows, width)],
            (middle, expand(into, []), down), "down", result=None,
        )[0]
    (total,) = call(
        lambda *refs: down_kernel([], *refs), [struct(rows, width, jnp.float32)],
        (middle, expand(into, []), down), "down",
    )
    z_in, x_early, y_late, total = after((z_in, x_early, y_late, total))
    pieces = crossed(share_in, y_in) + crossed(share_in, z_in, 2)
    pieces_down = crossed(share_early, y_early) + crossed(share_early, x_early, 2) + crossed(share_late, y_late)
    hidden = expand(None, pieces)
    return call(
        lambda *refs: last_kernel(plan(pieces_down), *refs), [struct(rows, width)],
        (total, hidden, *arrays(pieces_down)), "down",
        [pltpu.VMEM((rows, width), jnp.bfloat16), pltpu.SemaphoreType.DMA((rows // WIN,))], result=HBM,
    )[0]


def solution(mesh):
    in_specs = (
        P(("gx", "gy", "fsdp"), None),
        P(),
        P(),
        P("fsdp", None),
        P("fsdp", None),
        P("fsdp", None),
        P("fsdp", None),
        P(("gx", "gy", "fsdp")),
        P(("gx", "gy", "fsdp")),
        P(("gx", "gy", "fsdp"), None),
        P(("gx", "gy", "fsdp")),
    )
    out_specs = P(("gx", "gy", "fsdp"), None)
    return jax.shard_map(body, mesh=mesh, in_specs=in_specs, out_specs=out_specs, check_vma=False)
```

```python
import typing

import jax
import jax.numpy as jnp
from jax import lax
from jax.experimental import pallas as pl
from jax.experimental.pallas import tpu as pltpu
from jax.sharding import PartitionSpec as P

HEADS = 16
WIN = 128
CTX = 128
LANES = 128
EPSILON = 1e-05
LOG2E = 1.4426950408889634

VMEM = pl.BlockSpec(memory_space=pltpu.VMEM)
SMEM = pl.BlockSpec(memory_space=pltpu.SMEM)
HBM = pl.BlockSpec(memory_space=pltpu.HBM)
PARAMS = pltpu.CompilerParams(vmem_limit_bytes=16 * 1024 * 1024)


def ring(value, axis):
    count = lax.axis_size(axis)
    return lax.ppermute(value, axis, [(source, (source + 1) % count) for source in range(count)])


def swap(value, axis, bit):
    count = lax.axis_size(axis)
    return lax.ppermute(value, axis, [(source, source ^ bit) for source in range(count)])


def dot_nt(left, right):
    return lax.dot_general(left, right, (((1,), (1,)), ((), ())), preferred_element_type=jnp.float32)


def dot_nn(left, right):
    return jnp.dot(left, right, preferred_element_type=jnp.float32)


def layer_norm(values, gain):
    values = values.astype(jnp.float32)
    center = values - jnp.mean(values, axis=-1, keepdims=True)
    spread = jnp.mean(center * center, axis=-1, keepdims=True)
    return (center * lax.rsqrt(spread + EPSILON) * gain).astype(jnp.bfloat16)


def pick_rows(indices, count):
    column = jnp.broadcast_to(indices.astype(jnp.float32), (LANES, LANES)).T
    lane = lax.broadcasted_iota(jnp.int32, (LANES, LANES), 1).astype(jnp.float32)
    blocks = [
        jnp.where(column == lane + float(first), 1.0, 0.0).astype(jnp.bfloat16)
        for first in range(0, count, LANES)
    ]
    return jnp.concatenate(blocks, axis=1)


def norm_kernel(tokens, gain, send_x, send_y, out_x, out_y, normed):
    rows = tokens.shape[0]
    block = tokens[...]
    out_x[...] = dot_nn(pick_rows(send_x[...], rows), block).astype(jnp.bfloat16)
    out_y[...] = dot_nn(pick_rows(send_y[...], rows), block).astype(jnp.bfloat16)
    normed[...] = layer_norm(block, gain[...])


def present(halo, axis):
    return jnp.where(lax.axis_index(axis) > 0, halo[...].astype(jnp.float32), 0.0)


def context_kernel(normed, halo_x, halo_y, gain, context, chosen):
    parts = [layer_norm(present(halo_x, "gx"), gain[...]), layer_norm(present(halo_y, "gy"), gain[...])]
    pool = jnp.concatenate([normed[...]] + parts, axis=0)
    for window in range(context.shape[0]):
        picked = dot_nn(pick_rows(context[pl.ds(window, 1), :], pool.shape[0]), pool)
        chosen[pl.ds(window * CTX, CTX), :] = picked.astype(jnp.bfloat16)


class Share(typing.NamedTuple):
    base: int
    axis: str
    stride: int
    rows: int

    def start(self, flip):
        core = lax.axis_index("gx") % 2
        index = {
            "core": lambda: core,
            "gx": lambda: lax.axis_index("gx"),
            "gy": lambda: (lax.axis_index("gy") % 2) * 2 + core,
        }[self.axis]()
        return self.base + (index ^ flip) * self.stride


def slice_kernel(groups, *refs):
    parts, sems = refs[-1 - len(groups) : -1], refs[-1]
    copies = []
    for part, group in zip(parts, groups):
        low = 0
        for share in group:
            start = pl.multiple_of(share.start(0), 32)
            source = refs[len(copies)].at[pl.ds(start, share.rows), :]
            copies.append(pltpu.make_async_copy(source, part.at[pl.ds(low, share.rows), :], sems.at[len(copies)]))
            low += share.rows
    for copy in copies:
        copy.start()
    for copy in copies:
        copy.wait()


def prepare_kernel(shares, *refs):
    count = len(shares)
    (tokens, gain_one, gain_two, send_x, send_y, context, lengths), refs = refs[:7], refs[7:]
    shards, refs = refs[:count], refs[count:]
    (held, one, two, chosen, filled, out_x, out_y, normed), refs = refs[:8], refs[8:]
    parts, (rows_x, rows_y, sizes, sems) = refs[:count], refs[count:]
    pairs = [(tokens, held), (gain_one, one), (send_x, rows_x), (send_y, rows_y)]
    for number, share in enumerate(shares):
        start = pl.multiple_of(share.start(0), 32)
        pairs.append((shards[number].at[pl.ds(start, share.rows), :], parts[number]))
    pairs += [(gain_two, two), (context, chosen), (lengths, sizes)]
    copies = [pltpu.make_async_copy(*pair, sems.at[number]) for number, pair in enumerate(pairs)]
    for copy in copies:
        copy.start()
    for copy in copies[:4]:
        copy.wait()
    norm_kernel(held, one, rows_x, rows_y, out_x, out_y, normed)
    for copy in copies[4:]:
        copy.wait()
    for window in range(filled.shape[0]):
        filled[pl.ds(window, 1), :] = jnp.full((1, LANES), sizes[window], jnp.int32)


def assemble(whole, own, pieces):
    if not pieces:
        whole[...] = own[...]
        return
    rank = lax.axis_index("fsdp")
    rows = own.shape[0]
    whole[pl.ds(pl.multiple_of(rank * rows, rows), rows), :] = own[...]
    for share, flip, value in pieces:
        start = pl.multiple_of((1 - rank) * rows + share.start(flip), 32)
        whole[pl.ds(start, share.rows), :] = value[...]


def project_kernel(plan, normed, chosen, shard, *refs):
    pieces = refs[: len(plan)]
    queries, own_keys, ctx_keys, own_values, ctx_values, w_qkv = refs[len(plan) :]
    width = normed.shape[1]
    assemble(w_qkv, shard, [(*where, piece) for where, piece in zip(plan, pieces)])
    own, ctx = normed[...], chosen[...]
    w_q, w_k, w_v = (w_qkv[pl.ds(part * width, width), :] for part in range(3))
    queries[...] = dot_nt(w_q, own).astype(jnp.bfloat16)
    own_keys[...] = dot_nt(own, w_k).astype(jnp.bfloat16)
    ctx_keys[...] = dot_nt(ctx, w_k).astype(jnp.bfloat16)
    own_values[...] = dot_nt(w_v, own).astype(jnp.bfloat16)
    ctx_values[...] = dot_nt(w_v, ctx).astype(jnp.bfloat16)


def attend_kernel(windows, filled, queries, own_keys, ctx_keys, own_values, ctx_values, mixed):
    width = queries.shape[0]
    head_size = width // HEADS
    group = LANES // head_size
    scale = head_size ** (-0.5) * LOG2E
    ready = []
    for window in windows:
        length = filled[window : window + 1, :]
        row_full = lax.broadcasted_iota(jnp.int32, (WIN, LANES), 0) < length
        slot_full = lax.broadcasted_iota(jnp.int32, (1, WIN), 1) < length
        own_ones = lax.broadcasted_iota(jnp.int32, (16, WIN), 1) < length
        ones = jnp.concatenate([jnp.where(own_ones, 1.0, 0.0), jnp.ones((16, CTX), jnp.float32)], axis=1)
        ready.append((slice(window * WIN, (window + 1) * WIN), row_full, slot_full, ones.astype(jnp.bfloat16)))

    def scores_of(number, first):
        rows, row_full, _, _ = ready[number]
        lanes = slice(first, first + LANES)
        own = jnp.where(row_full, own_keys[rows, lanes], ctx_keys[rows.start : rows.start + 1, lanes])
        keys = jnp.concatenate([own, ctx_keys[rows, lanes]], axis=0)
        parts = []
        for head in range(group):
            pad = [jnp.zeros((head_size, WIN), jnp.bfloat16)] * group
            pad[head] = queries[first + head * head_size : first + (head + 1) * head_size, rows]
            parts.append(jnp.concatenate(pad, axis=0))
        return dot_nn(keys, jnp.concatenate(parts, axis=1))

    def mix(number, first, scores):
        rows, _, slot_full, ones = ready[number]
        largest = jnp.max(scores, axis=0, keepdims=True)
        probs = jnp.exp2((scores - largest) * scale).astype(jnp.bfloat16)
        outs = []
        for head in range(0, group, 2):
            features = slice(first + head * head_size, first + (head + 2) * head_size)
            own = jnp.where(slot_full, own_values[features, rows], jnp.zeros((), jnp.bfloat16))
            values = jnp.concatenate([own, ctx_values[features, rows]], axis=1)
            sums = dot_nn(jnp.concatenate([values, ones], axis=0), probs[:, head * WIN : (head + 2) * WIN])
            for part in range(2):
                block = sums[:, part * WIN : (part + 1) * WIN]
                weight = 1.0 / block[2 * head_size : 2 * head_size + 1]
                outs.append(block[part * head_size : (part + 1) * head_size] * weight)
        mixed[number * WIN : (number + 1) * WIN, first : first + LANES] = (
            jnp.concatenate(outs, axis=0).T.astype(jnp.bfloat16)
        )

    waiting = []
    for item in [(number, first) for number in range(len(windows)) for first in range(0, width, LANES)]:
        waiting.append((item, scores_of(*item)))
        if len(waiting) > 2:
            done, scores = waiting.pop(0)
            mix(*done, scores)
    for done, scores in waiting:
        mix(*done, scores)


def finish_kernel(parts, plan, tokens, gain, shard, *refs):
    mixed, pieces = refs[:parts], refs[parts : parts + len(plan)]
    middle, second, w_out = refs[parts + len(plan) :]
    assemble(w_out, shard, [(*where, piece) for where, piece in zip(plan, pieces)])
    low = 0
    for block in mixed:
        rows = slice(low, low + block.shape[0])
        total = tokens[rows, :].astype(jnp.float32) + dot_nt(block[...], w_out[...])
        middle[rows, :] = total
        second[rows, :] = layer_norm(total, gain[...])
        low += block.shape[0]


def columns_of(plan, number, piece):
    if not plan:
        return slice(None)
    share, flip = plan[number]
    return pl.ds(pl.multiple_of(share.start(flip), LANES), share.rows)


def hidden_kernel(plan, second, *refs):
    hidden = refs[-1]
    for number, piece in enumerate(refs[:-1]):
        units = jax.nn.gelu(dot_nt(second[...], piece[...])).astype(jnp.bfloat16)
        hidden[:, columns_of(plan, number, piece)] = units


def feed_kernel(start, second, into, down, output):
    size = min(256, into.shape[0])
    total = start[...]
    waiting = []

    def add(low, product):
        return total + dot_nn(jax.nn.gelu(product).astype(jnp.bfloat16), down[low : low + size, :])

    for low in range(0, into.shape[0], size):
        waiting.append((low, dot_nt(second[...], into[low : low + size, :])))
        if len(waiting) > 1:
            total = add(*waiting.pop(0))
    output[...] = add(*waiting.pop(0)).astype(output.dtype)


def last_kernel(plan, start, hidden, *refs):
    pieces, output, held, sems = refs[: len(plan)], refs[-3], refs[-2], refs[-1]
    blocks = start.shape[0] // WIN
    copies = []
    for block in range(blocks):
        rows = slice(block * WIN, (block + 1) * WIN)
        total = start[rows, :]
        for number, piece in enumerate(pieces):
            total = total + dot_nn(hidden[rows, columns_of(plan, number, piece)], piece[...])
        held[rows, :] = total.astype(output.dtype)
        copies.append(pltpu.make_async_copy(held.at[rows, :], output.at[rows, :], sems.at[block]))
        copies[-1].start()
    for copy in copies:
        copy.wait()


COSTS = {"norm": 1, "slices": 1, "prepare": 1, "context": 1, "project": 1, "attend": 50, "finish": 1, "feed": 1, "hidden": 1, "last": 1}


def call(kernel, outs, operands, name, scratch=(), specs=None, result=VMEM):
    specs = specs or [VMEM] * len(operands)
    placed = [
        pltpu.with_memory_space_constraint(operand, pltpu.HBM) if spec is HBM else operand
        for operand, spec in zip(operands, specs)
    ]
    if result is VMEM:
        outs = [pltpu.VMEM(out.shape, out.dtype) for out in outs]
    return pl.pallas_call(
        kernel,
        out_shape=tuple(outs),
        in_specs=specs,
        out_specs=tuple(result or VMEM for _ in outs),
        scratch_shapes=list(scratch),
        compiler_params=PARAMS,
        name=name,
        cost_estimate=pl.CostEstimate(flops=COSTS[name] * 10**7, bytes_accessed=0, transcendentals=0),
    )(*placed)


def struct(rows, width, dtype=jnp.bfloat16):
    return jax.ShapeDtypeStruct((rows, width), dtype)


def body(tokens, gain_one, gain_two, w_qkv, w_out, w_in, w_down, send_x, send_y, context, lengths):
    rows, width = tokens.shape
    halo = send_x.shape[0]
    gain_one, gain_two = gain_one[None, :], gain_two[None, :]
    send_x, send_y = send_x[None, :], send_y[None, :]
    after = lax.optimization_barrier
    paired = lax.axis_size("fsdp") == 2 and lax.axis_size("gx") == 4 and lax.axis_size("gy") % 2 == 0
    edges = [struct(halo, width), struct(halo, width), struct(rows, width)]

    if not paired:
        qkv, out, into, down = (
            lax.all_gather(weight, "fsdp", axis=0, tiled=True) for weight in (w_qkv, w_out, w_in, w_down)
        )
        out_x, out_y, normed = call(norm_kernel, edges, (tokens, gain_one, send_x, send_y), "norm")
        filled = jnp.broadcast_to(lengths[:, None], context.shape)
    else:
        qkv, out, into, down = w_qkv, w_out, w_in, w_down
        size = qkv.shape[0] // 2
        share_qkv = Share(0, "core", size, size)
        share_out = Share(0, "core", out.shape[0] // 2, out.shape[0] // 2)
        share_in = Share(0, "gy", into.shape[0] // 4, into.shape[0] // 4)
        size = down.shape[0] // 8
        share_early = Share(0, "gx", size, size)
        share_late = Share(4 * size, "core", 2 * size, 2 * size)
        tokens, gain_one, gain_two, context, filled, out_x, out_y, normed, part_qkv = call(
            lambda *refs: prepare_kernel([share_qkv], *refs),
            [
                struct(rows, width), struct(1, width, jnp.float32), struct(1, width, jnp.float32),
                struct(*context.shape, jnp.int32), struct(*context.shape, jnp.int32),
            ]
            + edges + [struct(share_qkv.rows, width)],
            (tokens, gain_one, gain_two, send_x, send_y, context, lengths, qkv), "prepare",
            [
                pltpu.VMEM(send_x.shape, jnp.int32), pltpu.VMEM(send_y.shape, jnp.int32),
                pltpu.SMEM(lengths.shape, jnp.int32), pltpu.SemaphoreType.DMA((8,)),
            ],
            [HBM] * 8,
        )
        y_qkv = swap(part_qkv, "fsdp", 1)
        groups = [[share_in], [share_out, share_early], [share_late]]
        later, normed = after(((w_in, w_out, w_down), normed))
        parts = call(
            lambda *refs: slice_kernel(groups, *refs),
            [struct(sum(share.rows for share in group), width) for group in groups],
            (later[0], later[1], later[2], later[2]), "slices", [pltpu.SemaphoreType.DMA((4,))], [HBM] * 4,
        )
        y_in, y_middle, y_late = (swap(part, "fsdp", 1) for part in parts)

    def crossed(share, near, flip=0):
        return [(share, flip, near), (share, flip + 1, swap(near, "gx", 1))]

    def arrays(pieces):
        return [piece[2] for piece in pieces]

    def plan(pieces):
        return [piece[:2] for piece in pieces]

    halo_x = ring(out_x, "gx")
    halo_y = ring(out_y, "gy")
    (chosen,) = call(context_kernel, [struct(rows, width)], (normed, halo_x, halo_y, gain_one, context), "context")
    if paired:
        y_qkv, chosen = after((y_qkv, chosen))
    pieces = []
    if paired:
        pieces.append((share_qkv, 0, y_qkv))
        size = share_qkv.rows // 2
        for low in range(0, share_qkv.rows, size):
            share = share_qkv._replace(base=low, rows=size)
            pieces.append((share, 1, swap(y_qkv[low : low + size], "gx", 1)))
    projected = call(
        lambda *refs, plan=plan(pieces): project_kernel(plan, *refs), [struct(rows, width)] * 5,
        (normed, chosen, qkv, *arrays(pieces)), "project", [pltpu.VMEM((3 * width, width), jnp.bfloat16)],
    )

    def attend(windows):
        return call(
            lambda *refs: attend_kernel(windows, *refs), [struct(len(windows) * WIN, width)],
            (filled, *projected), "attend",
        )

    windows = list(range(rows // WIN))
    half = len(windows) // 2
    mixed = attend(windows[:half])
    pieces_out, pieces_in, pieces_down, pieces_last = [], [], [], []
    if paired:
        y_in, mixed = after((y_in, mixed))
        z_in = swap(y_in, "gy", 1)
        projected, y_in = after((projected, y_in))
    mixed += attend(windows[half:])
    if paired:
        y_middle, mixed = after((y_middle, mixed))
        y_out, y_early = y_middle[: share_out.rows], y_middle[share_out.rows :]
        pieces_out = crossed(share_out, y_out)
        x_early = swap(y_early, "gx", 2)
    middle, second = call(
        lambda *refs: finish_kernel(len(mixed), plan(pieces_out), *refs),
        [struct(rows, width, jnp.float32), struct(rows, width)], (tokens, gain_two, out, *mixed, *arrays(pieces_out)),
        "finish", [pltpu.VMEM((width, width), jnp.bfloat16)],
    )

    (total,) = call(
        feed_kernel, [struct(rows, width, jnp.float32 if paired else jnp.bfloat16)], (middle, second, into, down), "feed"
    )
    if not paired:
        return total
    z_in, total = after((z_in, total))
    pieces = crossed(share_in, y_in) + crossed(share_in, z_in, 2)
    (hidden,) = call(
        lambda *refs, plan=plan(pieces): hidden_kernel(plan, *refs), [struct(rows, into.shape[0])],
        (second, *arrays(pieces)), "hidden",
    )
    LATE = 0
    if LATE == 0:
        x_early, y_late, total = after((x_early, y_late, total))
    elif LATE == 1:
        x_early, y_late, hidden = after((x_early, y_late, hidden))
    else:
        y_late, total = after((y_late, total))
        x_early, hidden = after((x_early, hidden))
    pieces = crossed(share_early, y_early) + crossed(share_early, x_early, 2) + crossed(share_late, y_late)
    return call(
        lambda *refs: last_kernel(plan(pieces), *refs), [struct(rows, width)],
        (total, hidden, *arrays(pieces)), "last",
        [pltpu.VMEM((rows, width), jnp.bfloat16), pltpu.SemaphoreType.DMA((rows // WIN,))], result=HBM,
    )[0]


def solution(mesh):
    in_specs = (
        P(("gx", "gy", "fsdp"), None),
        P(),
        P(),
        P("fsdp", None),
        P("fsdp", None),
        P("fsdp", None),
        P("fsdp", None),
        P(("gx", "gy", "fsdp")),
        P(("gx", "gy", "fsdp")),
        P(("gx", "gy", "fsdp"), None),
        P(("gx", "gy", "fsdp")),
    )
    out_specs = P(("gx", "gy", "fsdp"), None)
    return jax.shard_map(body, mesh=mesh, in_specs=in_specs, out_specs=out_specs, check_vma=False)
```

```python
import typing

import jax
import jax.numpy as jnp
from jax import lax
from jax.experimental import pallas as pl
from jax.experimental.pallas import tpu as pltpu
from jax.sharding import PartitionSpec as P

HEADS = 16
WIN = 128
CTX = 128
LANES = 128
EPSILON = 1e-05
LOG2E = 1.4426950408889634

VMEM = pl.BlockSpec(memory_space=pltpu.VMEM)
SMEM = pl.BlockSpec(memory_space=pltpu.SMEM)
HBM = pl.BlockSpec(memory_space=pltpu.HBM)
PARAMS = pltpu.CompilerParams(vmem_limit_bytes=16 * 1024 * 1024)


def ring(value, axis):
    count = lax.axis_size(axis)
    return lax.ppermute(value, axis, [(source, (source + 1) % count) for source in range(count)])


def swap(value, axis, bit):
    count = lax.axis_size(axis)
    return lax.ppermute(value, axis, [(source, source ^ bit) for source in range(count)])


def dot_nt(left, right):
    return lax.dot_general(left, right, (((1,), (1,)), ((), ())), preferred_element_type=jnp.float32)


def dot_nn(left, right):
    return jnp.dot(left, right, preferred_element_type=jnp.float32)


def layer_norm(values, gain):
    values = values.astype(jnp.float32)
    center = values - jnp.mean(values, axis=-1, keepdims=True)
    spread = jnp.mean(center * center, axis=-1, keepdims=True)
    return (center * lax.rsqrt(spread + EPSILON) * gain).astype(jnp.bfloat16)


def pick_rows(indices, count):
    column = jnp.broadcast_to(indices.astype(jnp.float32), (LANES, LANES)).T
    lane = lax.broadcasted_iota(jnp.int32, (LANES, LANES), 1).astype(jnp.float32)
    blocks = [
        jnp.where(column == lane + float(first), 1.0, 0.0).astype(jnp.bfloat16)
        for first in range(0, count, LANES)
    ]
    return jnp.concatenate(blocks, axis=1)


def norm_kernel(tokens, gain, send_x, send_y, out_x, out_y, normed):
    rows = tokens.shape[0]
    block = tokens[...]
    out_x[...] = dot_nn(pick_rows(send_x[...], rows), block).astype(jnp.bfloat16)
    out_y[...] = dot_nn(pick_rows(send_y[...], rows), block).astype(jnp.bfloat16)
    normed[...] = layer_norm(block, gain[...])


def present(halo, axis):
    return jnp.where(lax.axis_index(axis) > 0, halo[...].astype(jnp.float32), 0.0)


def context_kernel(normed, halo_x, halo_y, gain, context, into, down, chosen, held_into, held_down, sems):
    copies = [
        pltpu.make_async_copy(into, held_into, sems.at[0]), pltpu.make_async_copy(down, held_down, sems.at[1])
    ]
    for copy in copies:
        copy.start()
    parts = [layer_norm(present(halo_x, "gx"), gain[...]), layer_norm(present(halo_y, "gy"), gain[...])]
    pool = jnp.concatenate([normed[...]] + parts, axis=0)
    for window in range(context.shape[0]):
        picked = dot_nn(pick_rows(context[pl.ds(window, 1), :], pool.shape[0]), pool)
        chosen[pl.ds(window * CTX, CTX), :] = picked.astype(jnp.bfloat16)
    for copy in copies:
        copy.wait()


class Share(typing.NamedTuple):
    base: int
    axis: str
    stride: int
    rows: int

    def start(self, flip):
        core = lax.axis_index("gx") % 2
        index = {
            "core": lambda: core,
            "gx": lambda: lax.axis_index("gx"),
            "gy": lambda: (lax.axis_index("gy") % 2) * 2 + core,
        }[self.axis]()
        return self.base + (index ^ flip) * self.stride


def slice_kernel(groups, *refs):
    parts, sems = refs[-1 - len(groups) : -1], refs[-1]
    copies = []
    for part, group in zip(parts, groups):
        low = 0
        for share in group:
            start = pl.multiple_of(share.start(0), 32)
            source = refs[len(copies)].at[pl.ds(start, share.rows), :]
            copies.append(pltpu.make_async_copy(source, part.at[pl.ds(low, share.rows), :], sems.at[len(copies)]))
            low += share.rows
    for copy in copies:
        copy.start()
    for copy in copies:
        copy.wait()


def prepare_kernel(shares, *refs):
    count = len(shares)
    (tokens, gain_one, gain_two, send_x, send_y, context, lengths), refs = refs[:7], refs[7:]
    shards, refs = refs[:count], refs[count:]
    (held, one, two, chosen, filled, out_x, out_y, normed), refs = refs[:8], refs[8:]
    parts, (rows_x, rows_y, sizes, sems) = refs[:count], refs[count:]
    pairs = [(tokens, held), (gain_one, one), (send_x, rows_x), (send_y, rows_y)]
    for number, share in enumerate(shares):
        start = pl.multiple_of(share.start(0), 32)
        pairs.append((shards[number].at[pl.ds(start, share.rows), :], parts[number]))
    pairs += [(gain_two, two), (context, chosen), (lengths, sizes)]
    copies = [pltpu.make_async_copy(*pair, sems.at[number]) for number, pair in enumerate(pairs)]
    for copy in copies:
        copy.start()
    for copy in copies[:4]:
        copy.wait()
    norm_kernel(held, one, rows_x, rows_y, out_x, out_y, normed)
    for copy in copies[4:]:
        copy.wait()
    for window in range(filled.shape[0]):
        filled[pl.ds(window, 1), :] = jnp.full((1, LANES), sizes[window], jnp.int32)


def assemble(whole, own, pieces):
    if not pieces:
        whole[...] = own[...]
        return
    rank = lax.axis_index("fsdp")
    rows = own.shape[0]
    whole[pl.ds(pl.multiple_of(rank * rows, rows), rows), :] = own[...]
    for share, flip, value in pieces:
        start = pl.multiple_of((1 - rank) * rows + share.start(flip), 32)
        whole[pl.ds(start, share.rows), :] = value[...]


def project_kernel(plan, normed, chosen, shard, *refs):
    pieces = refs[: len(plan)]
    queries, own_keys, ctx_keys, own_values, ctx_values, w_qkv = refs[len(plan) :]
    width = normed.shape[1]
    assemble(w_qkv, shard, [(*where, piece) for where, piece in zip(plan, pieces)])
    own, ctx = normed[...], chosen[...]
    w_q, w_k, w_v = (w_qkv[pl.ds(part * width, width), :] for part in range(3))
    queries[...] = dot_nt(w_q, own).astype(jnp.bfloat16)
    own_keys[...] = dot_nt(own, w_k).astype(jnp.bfloat16)
    ctx_keys[...] = dot_nt(ctx, w_k).astype(jnp.bfloat16)
    own_values[...] = dot_nt(w_v, own).astype(jnp.bfloat16)
    ctx_values[...] = dot_nt(w_v, ctx).astype(jnp.bfloat16)


def attend_kernel(windows, filled, queries, own_keys, ctx_keys, own_values, ctx_values, mixed):
    width = queries.shape[0]
    head_size = width // HEADS
    group = LANES // head_size
    scale = head_size ** (-0.5) * LOG2E
    ready = []
    for window in windows:
        length = filled[window : window + 1, :]
        row_full = lax.broadcasted_iota(jnp.int32, (WIN, LANES), 0) < length
        slot_full = lax.broadcasted_iota(jnp.int32, (1, WIN), 1) < length
        own_ones = lax.broadcasted_iota(jnp.int32, (16, WIN), 1) < length
        ones = jnp.concatenate([jnp.where(own_ones, 1.0, 0.0), jnp.ones((16, CTX), jnp.float32)], axis=1)
        ready.append((slice(window * WIN, (window + 1) * WIN), row_full, slot_full, ones.astype(jnp.bfloat16)))

    def scores_of(number, first):
        rows, row_full, _, _ = ready[number]
        lanes = slice(first, first + LANES)
        own = jnp.where(row_full, own_keys[rows, lanes], ctx_keys[rows.start : rows.start + 1, lanes])
        keys = jnp.concatenate([own, ctx_keys[rows, lanes]], axis=0)
        parts = []
        for head in range(group):
            pad = [jnp.zeros((head_size, WIN), jnp.bfloat16)] * group
            pad[head] = queries[first + head * head_size : first + (head + 1) * head_size, rows]
            parts.append(jnp.concatenate(pad, axis=0))
        return dot_nn(keys, jnp.concatenate(parts, axis=1))

    def mix(number, first, scores):
        rows, _, slot_full, ones = ready[number]
        largest = jnp.max(scores, axis=0, keepdims=True)
        probs = jnp.exp2((scores - largest) * scale).astype(jnp.bfloat16)
        outs = []
        for head in range(0, group, 2):
            features = slice(first + head * head_size, first + (head + 2) * head_size)
            own = jnp.where(slot_full, own_values[features, rows], jnp.zeros((), jnp.bfloat16))
            values = jnp.concatenate([own, ctx_values[features, rows]], axis=1)
            sums = dot_nn(jnp.concatenate([values, ones], axis=0), probs[:, head * WIN : (head + 2) * WIN])
            for part in range(2):
                block = sums[:, part * WIN : (part + 1) * WIN]
                weight = 1.0 / block[2 * head_size : 2 * head_size + 1]
                outs.append(block[part * head_size : (part + 1) * head_size] * weight)
        mixed[number * WIN : (number + 1) * WIN, first : first + LANES] = (
            jnp.concatenate(outs, axis=0).T.astype(jnp.bfloat16)
        )

    waiting = []
    for item in [(number, first) for number in range(len(windows)) for first in range(0, width, LANES)]:
        waiting.append((item, scores_of(*item)))
        if len(waiting) > 2:
            done, scores = waiting.pop(0)
            mix(*done, scores)
    for done, scores in waiting:
        mix(*done, scores)


def finish_kernel(parts, plan, tokens, gain, shard, *refs):
    mixed, pieces = refs[:parts], refs[parts : parts + len(plan)]
    middle, second, w_out = refs[parts + len(plan) :]
    assemble(w_out, shard, [(*where, piece) for where, piece in zip(plan, pieces)])
    low = 0
    for block in mixed:
        rows = slice(low, low + block.shape[0])
        total = tokens[rows, :].astype(jnp.float32) + dot_nt(block[...], w_out[...])
        middle[rows, :] = total
        second[rows, :] = layer_norm(total, gain[...])
        low += block.shape[0]


def columns_of(plan, number, piece):
    if not plan:
        return slice(None)
    share, flip = plan[number]
    return pl.ds(pl.multiple_of(share.start(flip), LANES), share.rows)


def hidden_kernel(plan, second, *refs):
    hidden = refs[-1]
    for number, piece in enumerate(refs[:-1]):
        units = jax.nn.gelu(dot_nt(second[...], piece[...])).astype(jnp.bfloat16)
        hidden[:, columns_of(plan, number, piece)] = units


def feed_kernel(start, second, into, down, output):
    size = min(256, into.shape[0])
    total = start[...]
    waiting = []

    def add(low, product):
        return total + dot_nn(jax.nn.gelu(product).astype(jnp.bfloat16), down[low : low + size, :])

    for low in range(0, into.shape[0], size):
        waiting.append((low, dot_nt(second[...], into[low : low + size, :])))
        if len(waiting) > 1:
            total = add(*waiting.pop(0))
    output[...] = add(*waiting.pop(0)).astype(output.dtype)


def add_kernel(plan, start, hidden, piece, output):
    output[...] = start[...] + dot_nn(hidden[:, columns_of(plan, 0, piece)], piece[...])


def last_kernel(plan, start, hidden, *refs):
    pieces, output, held, sems = refs[: len(plan)], refs[-3], refs[-2], refs[-1]
    blocks = start.shape[0] // WIN
    copies = []
    for block in range(blocks):
        rows = slice(block * WIN, (block + 1) * WIN)
        total = start[rows, :]
        for number, piece in enumerate(pieces):
            total = total + dot_nn(hidden[rows, columns_of(plan, number, piece)], piece[...])
        held[rows, :] = total.astype(output.dtype)
        copies.append(pltpu.make_async_copy(held.at[rows, :], output.at[rows, :], sems.at[block]))
        copies[-1].start()
    for copy in copies:
        copy.wait()


COSTS = {"norm": 1, "slices": 1, "prepare": 1, "context": 1, "project": 20, "attend": 1, "finish": 1, "feed": 1, "hidden": 60, "add": 1, "last": 1}


def call(kernel, outs, operands, name, scratch=(), specs=None, result=VMEM):
    specs = specs or [VMEM] * len(operands)
    placed = [
        pltpu.with_memory_space_constraint(operand, pltpu.HBM) if spec is HBM else operand
        for operand, spec in zip(operands, specs)
    ]
    if result is VMEM:
        outs = [pltpu.VMEM(out.shape, out.dtype) for out in outs]
    return pl.pallas_call(
        kernel,
        out_shape=tuple(outs),
        in_specs=specs,
        out_specs=tuple(result or VMEM for _ in outs),
        scratch_shapes=list(scratch),
        compiler_params=PARAMS,
        name=name,
        cost_estimate=pl.CostEstimate(flops=COSTS[name] * 10**7, bytes_accessed=0, transcendentals=0),
    )(*placed)


def struct(rows, width, dtype=jnp.bfloat16):
    return jax.ShapeDtypeStruct((rows, width), dtype)


def body(tokens, gain_one, gain_two, w_qkv, w_out, w_in, w_down, send_x, send_y, context, lengths):
    rows, width = tokens.shape
    halo = send_x.shape[0]
    gain_one, gain_two = gain_one[None, :], gain_two[None, :]
    send_x, send_y = send_x[None, :], send_y[None, :]
    after = lax.optimization_barrier
    paired = lax.axis_size("fsdp") == 2 and lax.axis_size("gx") == 4 and lax.axis_size("gy") % 2 == 0
    edges = [struct(halo, width), struct(halo, width), struct(rows, width)]

    if not paired:
        qkv, out, into, down = (
            lax.all_gather(weight, "fsdp", axis=0, tiled=True) for weight in (w_qkv, w_out, w_in, w_down)
        )
        out_x, out_y, normed = call(norm_kernel, edges, (tokens, gain_one, send_x, send_y), "norm")
        filled = jnp.broadcast_to(lengths[:, None], context.shape)
    else:
        qkv, out, into, down = w_qkv, w_out, w_in, w_down
        size = qkv.shape[0] // 4
        share_qkv = Share(0, "gx", size, size)
        share_out = Share(0, "core", out.shape[0] // 2, out.shape[0] // 2)
        share_in = Share(0, "gy", into.shape[0] // 4, into.shape[0] // 4)
        share_down = Share(0, "core", down.shape[0] // 2, down.shape[0] // 2)
        tokens, gain_one, gain_two, context, filled, out_x, out_y, normed, part_qkv = call(
            lambda *refs: prepare_kernel([share_qkv], *refs),
            [
                struct(rows, width), struct(1, width, jnp.float32), struct(1, width, jnp.float32),
                struct(*context.shape, jnp.int32), struct(*context.shape, jnp.int32),
            ]
            + edges + [struct(share_qkv.rows, width)],
            (tokens, gain_one, gain_two, send_x, send_y, context, lengths, qkv), "prepare",
            [
                pltpu.VMEM(send_x.shape, jnp.int32), pltpu.VMEM(send_y.shape, jnp.int32),
                pltpu.SMEM(lengths.shape, jnp.int32), pltpu.SemaphoreType.DMA((8,)),
            ],
            [HBM] * 8,
        )
        y_qkv = swap(part_qkv, "fsdp", 1)
        groups = [[share_in, share_out], [share_down]]
        later, normed = after(((w_in, w_out, w_down), normed))
        parts = call(
            lambda *refs: slice_kernel(groups, *refs),
            [struct(sum(share.rows for share in group), width) for group in groups],
            later, "slices", [pltpu.SemaphoreType.DMA((3,))], [HBM] * 3,
        )
        y_middle, y_down = (swap(part, "fsdp", 1) for part in parts)

    def crossed(share, near, flip=0):
        return [(share, flip, near), (share, flip + 1, swap(near, "gx", 1))]

    def arrays(pieces):
        return [piece[2] for piece in pieces]

    def plan(pieces):
        return [piece[:2] for piece in pieces]

    halo_x = ring(out_x, "gx")
    halo_y = ring(out_y, "gy")
    chosen, into, down = call(
        context_kernel, [struct(rows, width), struct(*into.shape), struct(*down.shape)],
        (normed, halo_x, halo_y, gain_one, context, into, down), "context",
        [pltpu.SemaphoreType.DMA((2,))], [VMEM] * 5 + [HBM] * 2,
    )
    if paired:
        size = share_qkv.rows // 2
        x_qkv = [swap(y_qkv[low : low + size], "gx", 2) for low in range(0, share_qkv.rows, size)]
        x_qkv, chosen = after((x_qkv, chosen))
    pieces = []
    if paired:
        pieces = crossed(share_qkv, y_qkv)
        for number, piece in enumerate(x_qkv):
            pieces += crossed(share_qkv._replace(base=number * size, rows=size), piece, 2)
    projected = call(
        lambda *refs, plan=plan(pieces): project_kernel(plan, *refs), [struct(rows, width)] * 5,
        (normed, chosen, qkv, *arrays(pieces)), "project", [pltpu.VMEM((3 * width, width), jnp.bfloat16)],
    )

    if paired:
        y_middle, projected = after((y_middle, projected))
        y_in, y_out = y_middle[: share_in.rows], y_middle[share_in.rows :]
        size = share_in.rows // 2
        z_in = [swap(y_in[low : low + size], "gy", 1) for low in range(0, share_in.rows, size)]
        projected, y_in, y_out = after((projected, y_in, y_out))

    def attend(windows):
        return call(
            lambda *refs: attend_kernel(windows, *refs), [struct(len(windows) * WIN, width)],
            (filled, *projected), "attend",
        )

    windows = list(range(rows // WIN))
    half = len(windows) // 2
    mixed = attend(windows[:half])
    pieces_out, pieces_in, pieces_down, pieces_last = [], [], [], []
    mixed += attend(windows[half:])
    if paired:
        pieces_out = crossed(share_out, y_out)
    middle, second = call(
        lambda *refs: finish_kernel(len(mixed), plan(pieces_out), *refs),
        [struct(rows, width, jnp.float32), struct(rows, width)], (tokens, gain_two, out, *mixed, *arrays(pieces_out)),
        "finish", [pltpu.VMEM((width, width), jnp.bfloat16)],
    )

    (total,) = call(
        feed_kernel, [struct(rows, width, jnp.float32 if paired else jnp.bfloat16)], (middle, second, into, down), "feed"
    )
    if not paired:
        return total
    z_in, total = after((z_in, total))
    pieces = crossed(share_in, y_in)
    size = share_in.rows // 2
    for number, piece in enumerate(z_in):
        pieces += crossed(share_in._replace(base=number * size, rows=size), piece, 2)
    held, y_down = after((arrays(pieces), y_down))
    (hidden,) = call(
        lambda *refs, plan=plan(pieces): hidden_kernel(plan, *refs), [struct(rows, into.shape[0])], (second, *held), "hidden",
    )
    size = share_down.rows // 1
    halves = [
        (share_down._replace(base=low, rows=size), 1, swap(y_down[low : low + size], "gx", 1))
        for low in range(0, share_down.rows, size)
    ]
    (total,) = call(
        lambda *refs: add_kernel([(share_down, 0)], *refs), [struct(rows, width, jnp.float32)],
        (total, hidden, y_down), "add",
    )
    return call(
        lambda *refs: last_kernel(plan(halves), *refs), [struct(rows, width)],
        (total, hidden, *arrays(halves)), "last",
        [pltpu.VMEM((rows, width), jnp.bfloat16), pltpu.SemaphoreType.DMA((rows // WIN,))], result=HBM,
    )[0]


def solution(mesh):
    in_specs = (
        P(("gx", "gy", "fsdp"), None),
        P(),
        P(),
        P("fsdp", None),
        P("fsdp", None),
        P("fsdp", None),
        P("fsdp", None),
        P(("gx", "gy", "fsdp")),
        P(("gx", "gy", "fsdp")),
        P(("gx", "gy", "fsdp"), None),
        P(("gx", "gy", "fsdp")),
    )
    out_specs = P(("gx", "gy", "fsdp"), None)
    return jax.shard_map(body, mesh=mesh, in_specs=in_specs, out_specs=out_specs, check_vma=False)
```

```python
import typing

import jax
import jax.numpy as jnp
from jax import lax
from jax.experimental import pallas as pl
from jax.experimental.pallas import tpu as pltpu
from jax.sharding import PartitionSpec as P

HEADS = 16
WIN = 128
CTX = 128
LANES = 128
EPSILON = 1e-05
LOG2E = 1.4426950408889634

VMEM = pl.BlockSpec(memory_space=pltpu.VMEM)
SMEM = pl.BlockSpec(memory_space=pltpu.SMEM)
HBM = pl.BlockSpec(memory_space=pltpu.HBM)
PARAMS = pltpu.CompilerParams(vmem_limit_bytes=16 * 1024 * 1024)


def ring(value, axis):
    count = lax.axis_size(axis)
    return lax.ppermute(value, axis, [(source, (source + 1) % count) for source in range(count)])


def swap(value, axis, bit):
    count = lax.axis_size(axis)
    return lax.ppermute(value, axis, [(source, source ^ bit) for source in range(count)])


def dot_nt(left, right):
    return lax.dot_general(left, right, (((1,), (1,)), ((), ())), preferred_element_type=jnp.float32)


def dot_nn(left, right):
    return jnp.dot(left, right, preferred_element_type=jnp.float32)


def layer_norm(values, gain):
    values = values.astype(jnp.float32)
    center = values - jnp.mean(values, axis=-1, keepdims=True)
    spread = jnp.mean(center * center, axis=-1, keepdims=True)
    return (center * lax.rsqrt(spread + EPSILON) * gain).astype(jnp.bfloat16)


def pick_rows(indices, count):
    column = jnp.broadcast_to(indices.astype(jnp.float32), (LANES, LANES)).T
    lane = lax.broadcasted_iota(jnp.int32, (LANES, LANES), 1).astype(jnp.float32)
    blocks = [
        jnp.where(column == lane + float(first), 1.0, 0.0).astype(jnp.bfloat16)
        for first in range(0, count, LANES)
    ]
    return jnp.concatenate(blocks, axis=1)


def norm_kernel(tokens, gain, send_x, send_y, out_x, out_y, normed):
    rows = tokens.shape[0]
    block = tokens[...]
    out_x[...] = dot_nn(pick_rows(send_x[...], rows), block).astype(jnp.bfloat16)
    out_y[...] = dot_nn(pick_rows(send_y[...], rows), block).astype(jnp.bfloat16)
    normed[...] = layer_norm(block, gain[...])


def present(halo, axis):
    return jnp.where(lax.axis_index(axis) > 0, halo[...].astype(jnp.float32), 0.0)


def context_kernel(normed, halo_x, halo_y, gain, context, into, down, chosen, held_into, held_down, sems):
    copies = [
        pltpu.make_async_copy(into, held_into, sems.at[0]), pltpu.make_async_copy(down, held_down, sems.at[1])
    ]
    for copy in copies:
        copy.start()
    parts = [layer_norm(present(halo_x, "gx"), gain[...]), layer_norm(present(halo_y, "gy"), gain[...])]
    pool = jnp.concatenate([normed[...]] + parts, axis=0)
    for window in range(context.shape[0]):
        picked = dot_nn(pick_rows(context[pl.ds(window, 1), :], pool.shape[0]), pool)
        chosen[pl.ds(window * CTX, CTX), :] = picked.astype(jnp.bfloat16)
    for copy in copies:
        copy.wait()


class Share(typing.NamedTuple):
    base: int
    axis: str
    stride: int
    rows: int

    def start(self, flip):
        core = lax.axis_index("gx") % 2
        index = {
            "core": lambda: core,
            "gx": lambda: lax.axis_index("gx"),
            "gy": lambda: (lax.axis_index("gy") % 2) * 2 + core,
        }[self.axis]()
        return self.base + (index ^ flip) * self.stride


def slice_kernel(groups, *refs):
    parts, sems = refs[-1 - len(groups) : -1], refs[-1]
    copies = []
    for part, group in zip(parts, groups):
        low = 0
        for share in group:
            start = pl.multiple_of(share.start(0), 32)
            source = refs[len(copies)].at[pl.ds(start, share.rows), :]
            copies.append(pltpu.make_async_copy(source, part.at[pl.ds(low, share.rows), :], sems.at[len(copies)]))
            low += share.rows
    for copy in copies:
        copy.start()
    for copy in copies:
        copy.wait()


def prepare_kernel(shares, *refs):
    count = len(shares)
    (tokens, gain_one, gain_two, send_x, send_y, context, lengths), refs = refs[:7], refs[7:]
    shards, refs = refs[:count], refs[count:]
    (held, one, two, chosen, filled, out_x, out_y, normed), refs = refs[:8], refs[8:]
    parts, (rows_x, rows_y, sizes, sems) = refs[:count], refs[count:]
    pairs = [(tokens, held), (gain_one, one), (send_x, rows_x), (send_y, rows_y)]
    for number, share in enumerate(shares):
        start = pl.multiple_of(share.start(0), 32)
        pairs.append((shards[number].at[pl.ds(start, share.rows), :], parts[number]))
    pairs += [(gain_two, two), (context, chosen), (lengths, sizes)]
    copies = [pltpu.make_async_copy(*pair, sems.at[number]) for number, pair in enumerate(pairs)]
    for copy in copies:
        copy.start()
    for copy in copies[:4]:
        copy.wait()
    norm_kernel(held, one, rows_x, rows_y, out_x, out_y, normed)
    for copy in copies[4:]:
        copy.wait()
    for window in range(filled.shape[0]):
        filled[pl.ds(window, 1), :] = jnp.full((1, LANES), sizes[window], jnp.int32)


def assemble(whole, own, pieces):
    if not pieces:
        whole[...] = own[...]
        return
    rank = lax.axis_index("fsdp")
    rows = own.shape[0]
    whole[pl.ds(pl.multiple_of(rank * rows, rows), rows), :] = own[...]
    for share, flip, value in pieces:
        start = pl.multiple_of((1 - rank) * rows + share.start(flip), 32)
        whole[pl.ds(start, share.rows), :] = value[...]


def project_kernel(plan, normed, chosen, shard, *refs):
    pieces = refs[: len(plan)]
    queries, own_keys, ctx_keys, own_values, ctx_values, w_qkv = refs[len(plan) :]
    width = normed.shape[1]
    assemble(w_qkv, shard, [(*where, piece) for where, piece in zip(plan, pieces)])
    own, ctx = normed[...], chosen[...]
    w_q, w_k, w_v = (w_qkv[pl.ds(part * width, width), :] for part in range(3))
    queries[...] = dot_nt(w_q, own).astype(jnp.bfloat16)
    own_keys[...] = dot_nt(own, w_k).astype(jnp.bfloat16)
    ctx_keys[...] = dot_nt(ctx, w_k).astype(jnp.bfloat16)
    own_values[...] = dot_nt(w_v, own).astype(jnp.bfloat16)
    ctx_values[...] = dot_nt(w_v, ctx).astype(jnp.bfloat16)


def attend_kernel(windows, filled, queries, own_keys, ctx_keys, own_values, ctx_values, mixed):
    width = queries.shape[0]
    head_size = width // HEADS
    group = LANES // head_size
    scale = head_size ** (-0.5) * LOG2E
    ready = []
    for window in windows:
        length = filled[window : window + 1, :]
        row_full = lax.broadcasted_iota(jnp.int32, (WIN, LANES), 0) < length
        slot_full = lax.broadcasted_iota(jnp.int32, (1, WIN), 1) < length
        own_ones = lax.broadcasted_iota(jnp.int32, (16, WIN), 1) < length
        ones = jnp.concatenate([jnp.where(own_ones, 1.0, 0.0), jnp.ones((16, CTX), jnp.float32)], axis=1)
        ready.append((slice(window * WIN, (window + 1) * WIN), row_full, slot_full, ones.astype(jnp.bfloat16)))

    def scores_of(number, first):
        rows, row_full, _, _ = ready[number]
        lanes = slice(first, first + LANES)
        own = jnp.where(row_full, own_keys[rows, lanes], ctx_keys[rows.start : rows.start + 1, lanes])
        keys = jnp.concatenate([own, ctx_keys[rows, lanes]], axis=0)
        parts = []
        for head in range(group):
            pad = [jnp.zeros((head_size, WIN), jnp.bfloat16)] * group
            pad[head] = queries[first + head * head_size : first + (head + 1) * head_size, rows]
            parts.append(jnp.concatenate(pad, axis=0))
        return dot_nn(keys, jnp.concatenate(parts, axis=1))

    def mix(number, first, scores):
        rows, _, slot_full, ones = ready[number]
        largest = jnp.max(scores, axis=0, keepdims=True)
        probs = jnp.exp2((scores - largest) * scale).astype(jnp.bfloat16)
        outs = []
        for head in range(0, group, 2):
            features = slice(first + head * head_size, first + (head + 2) * head_size)
            own = jnp.where(slot_full, own_values[features, rows], jnp.zeros((), jnp.bfloat16))
            values = jnp.concatenate([own, ctx_values[features, rows]], axis=1)
            sums = dot_nn(jnp.concatenate([values, ones], axis=0), probs[:, head * WIN : (head + 2) * WIN])
            for part in range(2):
                block = sums[:, part * WIN : (part + 1) * WIN]
                weight = 1.0 / block[2 * head_size : 2 * head_size + 1]
                outs.append(block[part * head_size : (part + 1) * head_size] * weight)
        mixed[number * WIN : (number + 1) * WIN, first : first + LANES] = (
            jnp.concatenate(outs, axis=0).T.astype(jnp.bfloat16)
        )

    waiting = []
    for item in [(number, first) for number in range(len(windows)) for first in range(0, width, LANES)]:
        waiting.append((item, scores_of(*item)))
        if len(waiting) > 2:
            done, scores = waiting.pop(0)
            mix(*done, scores)
    for done, scores in waiting:
        mix(*done, scores)


def finish_kernel(parts, plan, tokens, gain, shard, *refs):
    mixed, pieces = refs[:parts], refs[parts : parts + len(plan)]
    middle, second, w_out = refs[parts + len(plan) :]
    assemble(w_out, shard, [(*where, piece) for where, piece in zip(plan, pieces)])
    low = 0
    for block in mixed:
        rows = slice(low, low + block.shape[0])
        total = tokens[rows, :].astype(jnp.float32) + dot_nt(block[...], w_out[...])
        middle[rows, :] = total
        second[rows, :] = layer_norm(total, gain[...])
        low += block.shape[0]


def columns_of(plan, number, piece):
    if not plan:
        return slice(None)
    share, flip = plan[number]
    return pl.ds(pl.multiple_of(share.start(flip), LANES), share.rows)


def hidden_kernel(plan, second, *refs):
    hidden = refs[-1]
    for number, piece in enumerate(refs[:-1]):
        units = jax.nn.gelu(dot_nt(second[...], piece[...])).astype(jnp.bfloat16)
        hidden[:, columns_of(plan, number, piece)] = units


def feed_kernel(start, second, into, down, output):
    size = min(256, into.shape[0])
    total = start[...]
    waiting = []

    def add(low, product):
        return total + dot_nn(jax.nn.gelu(product).astype(jnp.bfloat16), down[low : low + size, :])

    for low in range(0, into.shape[0], size):
        waiting.append((low, dot_nt(second[...], into[low : low + size, :])))
        if len(waiting) > 1:
            total = add(*waiting.pop(0))
    output[...] = add(*waiting.pop(0)).astype(output.dtype)


def add_kernel(plan, start, hidden, *refs):
    total = start[...]
    for number, piece in enumerate(refs[:-1]):
        total = total + dot_nn(hidden[:, columns_of(plan, number, piece)], piece[...])
    refs[-1][...] = total


def last_kernel(plan, start, hidden, *refs):
    pieces, output, held, sems = refs[: len(plan)], refs[-3], refs[-2], refs[-1]
    blocks = start.shape[0] // WIN
    copies = []
    for block in range(blocks):
        rows = slice(block * WIN, (block + 1) * WIN)
        total = start[rows, :]
        for number, piece in enumerate(pieces):
            total = total + dot_nn(hidden[rows, columns_of(plan, number, piece)], piece[...])
        held[rows, :] = total.astype(output.dtype)
        copies.append(pltpu.make_async_copy(held.at[rows, :], output.at[rows, :], sems.at[block]))
        copies[-1].start()
    for copy in copies:
        copy.wait()


COSTS = {"norm": 1, "slices": 1, "prepare": 1, "context": 160, "project": 20, "attend": 20, "finish": 1, "feed": 1, "hidden": 1, "add": 1, "last": 1}


def call(kernel, outs, operands, name, scratch=(), specs=None, result=VMEM):
    specs = specs or [VMEM] * len(operands)
    placed = [
        pltpu.with_memory_space_constraint(operand, pltpu.HBM) if spec is HBM else operand
        for operand, spec in zip(operands, specs)
    ]
    if result is VMEM:
        outs = [pltpu.VMEM(out.shape, out.dtype) for out in outs]
    return pl.pallas_call(
        kernel,
        out_shape=tuple(outs),
        in_specs=specs,
        out_specs=tuple(result or VMEM for _ in outs),
        scratch_shapes=list(scratch),
        compiler_params=PARAMS,
        name=name,
        cost_estimate=pl.CostEstimate(flops=COSTS[name] * 10**7, bytes_accessed=0, transcendentals=0),
    )(*placed)


def struct(rows, width, dtype=jnp.bfloat16):
    return jax.ShapeDtypeStruct((rows, width), dtype)


def body(tokens, gain_one, gain_two, w_qkv, w_out, w_in, w_down, send_x, send_y, context, lengths):
    rows, width = tokens.shape
    halo = send_x.shape[0]
    gain_one, gain_two = gain_one[None, :], gain_two[None, :]
    send_x, send_y = send_x[None, :], send_y[None, :]
    after = lax.optimization_barrier
    paired = lax.axis_size("fsdp") == 2 and lax.axis_size("gx") == 4 and lax.axis_size("gy") % 2 == 0
    edges = [struct(halo, width), struct(halo, width), struct(rows, width)]

    if not paired:
        qkv, out, into, down = (
            lax.all_gather(weight, "fsdp", axis=0, tiled=True) for weight in (w_qkv, w_out, w_in, w_down)
        )
        out_x, out_y, normed = call(norm_kernel, edges, (tokens, gain_one, send_x, send_y), "norm")
        filled = jnp.broadcast_to(lengths[:, None], context.shape)
    else:
        qkv, out, into, down = w_qkv, w_out, w_in, w_down
        size = qkv.shape[0] // 4
        share_qkv = Share(0, "gx", size, size)
        share_out = Share(0, "core", out.shape[0] // 2, out.shape[0] // 2)
        share_in = Share(0, "gy", into.shape[0] // 4, into.shape[0] // 4)
        size = down.shape[0] // 8
        share_early = Share(0, "gx", size, size)
        share_late = Share(4 * size, "core", 2 * size, 2 * size)
        tokens, gain_one, gain_two, context, filled, out_x, out_y, normed, part_qkv = call(
            lambda *refs: prepare_kernel([share_qkv], *refs),
            [
                struct(rows, width), struct(1, width, jnp.float32), struct(1, width, jnp.float32),
                struct(*context.shape, jnp.int32), struct(*context.shape, jnp.int32),
            ]
            + edges + [struct(share_qkv.rows, width)],
            (tokens, gain_one, gain_two, send_x, send_y, context, lengths, qkv), "prepare",
            [
                pltpu.VMEM(send_x.shape, jnp.int32), pltpu.VMEM(send_y.shape, jnp.int32),
                pltpu.SMEM(lengths.shape, jnp.int32), pltpu.SemaphoreType.DMA((8,)),
            ],
            [HBM] * 8,
        )
        y_qkv = swap(part_qkv, "fsdp", 1)
        groups = [[share_in], [share_out, share_early], [share_late]]
        later, normed = after(((w_in, w_out, w_down), normed))
        parts = call(
            lambda *refs: slice_kernel(groups, *refs),
            [struct(sum(share.rows for share in group), width) for group in groups],
            (*later, later[2]), "slices", [pltpu.SemaphoreType.DMA((4,))], [HBM] * 4,
        )
        y_in, y_middle, y_late = (swap(part, "fsdp", 1) for part in parts)

    def crossed(share, near, flip=0):
        return [(share, flip, near), (share, flip + 1, swap(near, "gx", 1))]

    def arrays(pieces):
        return [piece[2] for piece in pieces]

    def plan(pieces):
        return [piece[:2] for piece in pieces]

    halo_x = ring(out_x, "gx")
    halo_y = ring(out_y, "gy")
    chosen, into, down = call(
        context_kernel, [struct(rows, width), struct(*into.shape), struct(*down.shape)],
        (normed, halo_x, halo_y, gain_one, context, into, down), "context",
        [pltpu.SemaphoreType.DMA((2,))], [VMEM] * 5 + [HBM] * 2,
    )
    if paired:
        x_qkv = swap(y_qkv, "gx", 2)
        x_qkv, y_in, chosen = after((x_qkv, y_in, chosen))
        z_in = swap(y_in, "gy", 1)
        if 1:
            chosen, y_in = after((chosen, y_in))
    pieces = []
    if paired:
        pieces = crossed(share_qkv, y_qkv) + [(share_qkv, 2, x_qkv)]
        size = share_qkv.rows // 1
        for low in range(0, share_qkv.rows, size):
            pieces.append((share_qkv._replace(base=low, rows=size), 3, swap(x_qkv[low : low + size], "gx", 1)))
    projected = call(
        lambda *refs, plan=plan(pieces): project_kernel(plan, *refs), [struct(rows, width)] * 5,
        (normed, chosen, qkv, *arrays(pieces)), "project", [pltpu.VMEM((3 * width, width), jnp.bfloat16)],
    )

    def attend(windows):
        return call(
            lambda *refs: attend_kernel(windows, *refs), [struct(len(windows) * WIN, width)],
            (filled, *projected), "attend",
        )

    windows = list(range(rows // WIN))
    half = len(windows) // 2
    mixed = attend(windows[:half])
    pieces_out, pieces_in, pieces_down, pieces_last = [], [], [], []
    if paired:
        y_middle, mixed = after((y_middle, mixed))
        y_out, y_early = y_middle[: share_out.rows], y_middle[share_out.rows :]
        x_early = swap(y_early, "gx", 2)
        projected, y_out, y_early = after((projected, y_out, y_early))
    mixed += attend(windows[half:])
    if paired:
        pieces_out = crossed(share_out, y_out)
        z_in, mixed = after((z_in, mixed))
    middle, second = call(
        lambda *refs: finish_kernel(len(mixed), plan(pieces_out), *refs),
        [struct(rows, width, jnp.float32), struct(rows, width)], (tokens, gain_two, out, *mixed, *arrays(pieces_out)),
        "finish", [pltpu.VMEM((width, width), jnp.bfloat16)],
    )

    (total,) = call(
        feed_kernel, [struct(rows, width, jnp.float32 if paired else jnp.bfloat16)], (middle, second, into, down), "feed"
    )
    if not paired:
        return total
    pieces = crossed(share_in, y_in)
    pieces += crossed(share_in, z_in, 2)
    held = arrays(pieces)
    x_early, y_late, total = after((x_early, y_late, total))
    (hidden,) = call(
        lambda *refs, plan=plan(pieces): hidden_kernel(plan, *refs), [struct(rows, into.shape[0])], (second, *held), "hidden",
    )
    first = crossed(share_early, y_early) + [(share_late, 0, y_late)]
    rest = crossed(share_early, x_early, 2) + [(share_late, 1, swap(y_late, "gx", 1))]
    (total,) = call(
        lambda *refs: add_kernel(plan(first), *refs), [struct(rows, width, jnp.float32)],
        (total, hidden, *arrays(first)), "add",
    )
    return call(
        lambda *refs: last_kernel(plan(rest), *refs), [struct(rows, width)],
        (total, hidden, *arrays(rest)), "last",
        [pltpu.VMEM((rows, width), jnp.bfloat16), pltpu.SemaphoreType.DMA((rows // WIN,))], result=HBM,
    )[0]


def solution(mesh):
    in_specs = (
        P(("gx", "gy", "fsdp"), None),
        P(),
        P(),
        P("fsdp", None),
        P("fsdp", None),
        P("fsdp", None),
        P("fsdp", None),
        P(("gx", "gy", "fsdp")),
        P(("gx", "gy", "fsdp")),
        P(("gx", "gy", "fsdp"), None),
        P(("gx", "gy", "fsdp")),
    )
    out_specs = P(("gx", "gy", "fsdp"), None)
    return jax.shard_map(body, mesh=mesh, in_specs=in_specs, out_specs=out_specs, check_vma=False)
```

```python
import typing

import jax
import jax.numpy as jnp
from jax import lax
from jax.experimental import pallas as pl
from jax.experimental.pallas import tpu as pltpu
from jax.sharding import PartitionSpec as P

HEADS = 16
WIN = 128
CTX = 128
LANES = 128
EPSILON = 1e-05
LOG2E = 1.4426950408889634

VMEM = pl.BlockSpec(memory_space=pltpu.VMEM)
SMEM = pl.BlockSpec(memory_space=pltpu.SMEM)
HBM = pl.BlockSpec(memory_space=pltpu.HBM)
PARAMS = pltpu.CompilerParams(vmem_limit_bytes=16 * 1024 * 1024)


def ring(value, axis):
    count = lax.axis_size(axis)
    return lax.ppermute(value, axis, [(source, (source + 1) % count) for source in range(count)])


def swap(value, axis, bit):
    count = lax.axis_size(axis)
    return lax.ppermute(value, axis, [(source, source ^ bit) for source in range(count)])


def dot_nt(left, right):
    return lax.dot_general(left, right, (((1,), (1,)), ((), ())), preferred_element_type=jnp.float32)


def dot_nn(left, right):
    return jnp.dot(left, right, preferred_element_type=jnp.float32)


def layer_norm(values, gain):
    values = values.astype(jnp.float32)
    center = values - jnp.mean(values, axis=-1, keepdims=True)
    spread = jnp.mean(center * center, axis=-1, keepdims=True)
    return (center * lax.rsqrt(spread + EPSILON) * gain).astype(jnp.bfloat16)


def pick_rows(indices, count):
    column = jnp.broadcast_to(indices.astype(jnp.float32), (LANES, LANES)).T
    lane = lax.broadcasted_iota(jnp.int32, (LANES, LANES), 1).astype(jnp.float32)
    blocks = [
        jnp.where(column == lane + float(first), 1.0, 0.0).astype(jnp.bfloat16)
        for first in range(0, count, LANES)
    ]
    return jnp.concatenate(blocks, axis=1)


def pick_kernel(tokens, send_x, send_y, out_x, out_y):
    rows = tokens.shape[0]
    block = tokens[...]
    out_x[...] = dot_nn(pick_rows(send_x[...], rows), block).astype(jnp.bfloat16)
    out_y[...] = dot_nn(pick_rows(send_y[...], rows), block).astype(jnp.bfloat16)


def present(halo, axis):
    return jnp.where(lax.axis_index(axis) > 0, halo[...].astype(jnp.float32), 0.0)


def context_rows(tokens, halo_x, halo_y, gain, context, normed, chosen):
    normed[...] = layer_norm(tokens[...], gain[...])
    parts = [layer_norm(present(halo_x, "gx"), gain[...]), layer_norm(present(halo_y, "gy"), gain[...])]
    pool = jnp.concatenate([normed[...]] + parts, axis=0)
    for window in range(context.shape[0]):
        picked = dot_nn(pick_rows(context[pl.ds(window, 1), :], pool.shape[0]), pool)
        chosen[pl.ds(window * CTX, CTX), :] = picked.astype(jnp.bfloat16)


def project_half(second, weights, own, ctx, queries, own_keys, ctx_keys, own_values, ctx_values):
    width = own.shape[1]
    half = width // 2
    rows, others = own[...], ctx[...]
    if second:
        columns, w_k = slice(half, width), weights[:half, :]
        own_values[...] = dot_nt(weights[half:, :], rows).astype(jnp.bfloat16)
        ctx_values[...] = dot_nt(weights[half:, :], others).astype(jnp.bfloat16)
    else:
        columns, w_k = slice(0, half), weights[width:, :]
        queries[...] = dot_nt(weights[:width, :], rows).astype(jnp.bfloat16)
    own_keys[:, columns] = dot_nt(rows, w_k).astype(jnp.bfloat16)
    ctx_keys[:, columns] = dot_nt(others, w_k).astype(jnp.bfloat16)


def context_kernel(tokens, halo_x, halo_y, gain, context, qkv, into, down, normed, chosen, *refs):
    projected, (held_into, held_down, held_qkv, sems) = refs[:5], refs[5:]
    copies = [
        pltpu.make_async_copy(source, target, sems.at[number])
        for number, (source, target) in enumerate([(qkv, held_qkv), (into, held_into), (down, held_down)])
    ]
    for copy in copies:
        copy.start()
    context_rows(tokens, halo_x, halo_y, gain, context, normed, chosen)
    copies[0].wait()
    for rank in range(2):
        @pl.when(lax.axis_index("fsdp") == rank)
        def _(rank=rank):
            project_half(rank == 1, held_qkv, normed, chosen, *projected)
    for copy in copies[1:]:
        copy.wait()


def project_rest_kernel(plan, normed, chosen, *refs):
    pieces, refs = refs[: len(plan)], refs[len(plan) + 5 :]
    projected, whole = refs[:5], refs[5]
    for (share, flip), piece in zip(plan, pieces):
        start = pl.multiple_of(share.start(flip), 32)
        whole[pl.ds(start, share.rows), :] = piece[...]
    for rank in range(2):
        @pl.when(lax.axis_index("fsdp") == rank)
        def _(rank=rank):
            project_half(rank == 0, whole, normed, chosen, *projected)


class Share(typing.NamedTuple):
    base: int
    axis: str
    stride: int
    rows: int

    def start(self, flip):
        core = lax.axis_index("gx") % 2
        index = {
            "core": lambda: core,
            "gx": lambda: lax.axis_index("gx"),
            "gy": lambda: (lax.axis_index("gy") % 2) * 2 + core,
        }[self.axis]()
        return self.base + (index ^ flip) * self.stride


def slice_kernel(groups, *refs):
    parts, sems = refs[-1 - len(groups) : -1], refs[-1]
    copies = []
    for part, group in zip(parts, groups):
        low = 0
        for share in group:
            start = pl.multiple_of(share.start(0), 32)
            source = refs[len(copies)].at[pl.ds(start, share.rows), :]
            copies.append(pltpu.make_async_copy(source, part.at[pl.ds(low, share.rows), :], sems.at[len(copies)]))
            low += share.rows
    for copy in copies:
        copy.start()
    for copy in copies:
        copy.wait()


def prepare_kernel(shares, *refs):
    count = len(shares)
    (tokens, gain_one, gain_two, send_x, send_y, context, lengths), refs = refs[:7], refs[7:]
    shards, refs = refs[:count], refs[count:]
    (held, one, two, chosen, filled, out_x, out_y), refs = refs[:7], refs[7:]
    parts, (rows_x, rows_y, sizes, sems) = refs[:count], refs[count:]
    pairs = [(tokens, held), (send_x, rows_x), (send_y, rows_y)]
    for number, share in enumerate(shares):
        start = pl.multiple_of(share.start(0), 32)
        pairs.append((shards[number].at[pl.ds(start, share.rows), :], parts[number]))
    pairs += [(gain_one, one), (gain_two, two), (context, chosen), (lengths, sizes)]
    copies = [pltpu.make_async_copy(*pair, sems.at[number]) for number, pair in enumerate(pairs)]
    for copy in copies:
        copy.start()
    for copy in copies[:3]:
        copy.wait()
    pick_kernel(held, rows_x, rows_y, out_x, out_y)
    for copy in copies[3:]:
        copy.wait()
    for window in range(filled.shape[0]):
        filled[pl.ds(window, 1), :] = jnp.full((1, LANES), sizes[window], jnp.int32)


def assemble(whole, own, pieces):
    if not pieces:
        whole[...] = own[...]
        return
    rank = lax.axis_index("fsdp")
    rows = own.shape[0]
    whole[pl.ds(pl.multiple_of(rank * rows, rows), rows), :] = own[...]
    for share, flip, value in pieces:
        start = pl.multiple_of((1 - rank) * rows + share.start(flip), 32)
        whole[pl.ds(start, share.rows), :] = value[...]


def project_kernel(normed, chosen, w_qkv, queries, own_keys, ctx_keys, own_values, ctx_values):
    width = normed.shape[1]
    own, ctx = normed[...], chosen[...]
    w_q, w_k, w_v = (w_qkv[pl.ds(part * width, width), :] for part in range(3))
    queries[...] = dot_nt(w_q, own).astype(jnp.bfloat16)
    own_keys[...] = dot_nt(own, w_k).astype(jnp.bfloat16)
    ctx_keys[...] = dot_nt(ctx, w_k).astype(jnp.bfloat16)
    own_values[...] = dot_nt(w_v, own).astype(jnp.bfloat16)
    ctx_values[...] = dot_nt(w_v, ctx).astype(jnp.bfloat16)


def attend_kernel(windows, filled, queries, own_keys, ctx_keys, own_values, ctx_values, mixed):
    width = queries.shape[0]
    head_size = width // HEADS
    group = LANES // head_size
    scale = head_size ** (-0.5) * LOG2E
    ready = []
    for window in windows:
        length = filled[window : window + 1, :]
        row_full = lax.broadcasted_iota(jnp.int32, (WIN, LANES), 0) < length
        slot_full = lax.broadcasted_iota(jnp.int32, (1, WIN), 1) < length
        own_ones = lax.broadcasted_iota(jnp.int32, (16, WIN), 1) < length
        ones = jnp.concatenate([jnp.where(own_ones, 1.0, 0.0), jnp.ones((16, CTX), jnp.float32)], axis=1)
        ready.append((slice(window * WIN, (window + 1) * WIN), row_full, slot_full, ones.astype(jnp.bfloat16)))

    def scores_of(number, first):
        rows, row_full, _, _ = ready[number]
        lanes = slice(first, first + LANES)
        own = jnp.where(row_full, own_keys[rows, lanes], ctx_keys[rows.start : rows.start + 1, lanes])
        keys = jnp.concatenate([own, ctx_keys[rows, lanes]], axis=0)
        parts = []
        for head in range(group):
            pad = [jnp.zeros((head_size, WIN), jnp.bfloat16)] * group
            pad[head] = queries[first + head * head_size : first + (head + 1) * head_size, rows]
            parts.append(jnp.concatenate(pad, axis=0))
        return dot_nn(keys, jnp.concatenate(parts, axis=1))

    def mix(number, first, scores):
        rows, _, slot_full, ones = ready[number]
        largest = jnp.max(scores, axis=0, keepdims=True)
        probs = jnp.exp2((scores - largest) * scale).astype(jnp.bfloat16)
        outs = []
        for head in range(0, group, 2):
            features = slice(first + head * head_size, first + (head + 2) * head_size)
            own = jnp.where(slot_full, own_values[features, rows], jnp.zeros((), jnp.bfloat16))
            values = jnp.concatenate([own, ctx_values[features, rows]], axis=1)
            sums = dot_nn(jnp.concatenate([values, ones], axis=0), probs[:, head * WIN : (head + 2) * WIN])
            for part in range(2):
                block = sums[:, part * WIN : (part + 1) * WIN]
                weight = 1.0 / block[2 * head_size : 2 * head_size + 1]
                outs.append(block[part * head_size : (part + 1) * head_size] * weight)
        mixed[number * WIN : (number + 1) * WIN, first : first + LANES] = (
            jnp.concatenate(outs, axis=0).T.astype(jnp.bfloat16)
        )

    waiting = []
    for item in [(number, first) for number in range(len(windows)) for first in range(0, width, LANES)]:
        waiting.append((item, scores_of(*item)))
        if len(waiting) > 2:
            done, scores = waiting.pop(0)
            mix(*done, scores)
    for done, scores in waiting:
        mix(*done, scores)


def finish_kernel(parts, plan, tokens, gain, shard, *refs):
    mixed, pieces = refs[:parts], refs[parts : parts + len(plan)]
    middle, second, w_out = refs[parts + len(plan) :]
    assemble(w_out, shard, [(*where, piece) for where, piece in zip(plan, pieces)])
    low = 0
    for block in mixed:
        rows = slice(low, low + block.shape[0])
        total = tokens[rows, :].astype(jnp.float32) + dot_nt(block[...], w_out[...])
        middle[rows, :] = total
        second[rows, :] = layer_norm(total, gain[...])
        low += block.shape[0]


def columns_of(plan, number, piece):
    if not plan:
        return slice(None)
    share, flip = plan[number]
    return pl.ds(pl.multiple_of(share.start(flip), LANES), share.rows)


def hidden_kernel(plan_in, plan_down, start, second, *refs):
    into, down, (hidden, total) = refs[: len(plan_in)], refs[len(plan_in) : -2], refs[-2:]
    waiting = []

    def keep(number, product):
        hidden[:, columns_of(plan_in, number, into[number])] = jax.nn.gelu(product).astype(jnp.bfloat16)

    for number, piece in enumerate(into):
        waiting.append((number, dot_nt(second[...], piece[...])))
        if len(waiting) > 1:
            keep(*waiting.pop(0))
    keep(*waiting.pop(0))
    units = [hidden[:, columns_of(plan_down, number, piece)] for number, piece in enumerate(down)]
    weights = jnp.concatenate([piece[...] for piece in down], axis=0)
    total[...] = start[...] + dot_nn(jnp.concatenate(units, axis=1), weights)


def feed_kernel(start, second, into, down, output):
    size = min(256, into.shape[0])
    total = start[...]
    waiting = []

    def add(low, product):
        return total + dot_nn(jax.nn.gelu(product).astype(jnp.bfloat16), down[low : low + size, :])

    for low in range(0, into.shape[0], size):
        waiting.append((low, dot_nt(second[...], into[low : low + size, :])))
        if len(waiting) > 1:
            total = add(*waiting.pop(0))
    output[...] = add(*waiting.pop(0)).astype(output.dtype)


def last_kernel(plan, start, hidden, *refs):
    pieces, output, held, sems = refs[: len(plan)], refs[-3], refs[-2], refs[-1]
    weights = jnp.concatenate([piece[...] for piece in pieces], axis=0)
    blocks = sems.shape[0]
    size = start.shape[0] // blocks
    copies = []
    for block in range(blocks):
        rows = slice(block * size, (block + 1) * size)
        units = [hidden[rows, columns_of(plan, number, piece)] for number, piece in enumerate(pieces)]
        total = start[rows, :] + dot_nn(jnp.concatenate(units, axis=1), weights)
        held[rows, :] = total.astype(output.dtype)
        copies.append(pltpu.make_async_copy(held.at[rows, :], output.at[rows, :], sems.at[block]))
        copies[-1].start()
    for copy in copies:
        copy.wait()


COSTS = {"pick": 1, "slices": 1, "prepare": 1, "context": 160, "project": 20, "attend": 20, "finish": 1, "feed": 1, "hidden": 1, "last": 1}


def call(kernel, outs, operands, name, scratch=(), specs=None, result=VMEM, aliases={}):
    specs = specs or [VMEM] * len(operands)
    placed = [
        pltpu.with_memory_space_constraint(operand, pltpu.HBM) if spec is HBM else operand
        for operand, spec in zip(operands, specs)
    ]
    if result is VMEM:
        outs = [pltpu.VMEM(out.shape, out.dtype) for out in outs]
    return pl.pallas_call(
        kernel,
        out_shape=tuple(outs),
        in_specs=specs,
        out_specs=tuple(result or VMEM for _ in outs),
        scratch_shapes=list(scratch),
        compiler_params=PARAMS,
        name=name,
        input_output_aliases=aliases,
        cost_estimate=pl.CostEstimate(flops=COSTS[name] * 10**7, bytes_accessed=0, transcendentals=0),
    )(*placed)


def struct(rows, width, dtype=jnp.bfloat16):
    return jax.ShapeDtypeStruct((rows, width), dtype)


def body(tokens, gain_one, gain_two, w_qkv, w_out, w_in, w_down, send_x, send_y, context, lengths):
    rows, width = tokens.shape
    halo = send_x.shape[0]
    gain_one, gain_two = gain_one[None, :], gain_two[None, :]
    send_x, send_y = send_x[None, :], send_y[None, :]
    after = lax.optimization_barrier
    paired = lax.axis_size("fsdp") == 2 and lax.axis_size("gx") == 4 and lax.axis_size("gy") % 2 == 0
    edges = [struct(halo, width), struct(halo, width)]

    if not paired:
        qkv, out, into, down = (
            lax.all_gather(weight, "fsdp", axis=0, tiled=True) for weight in (w_qkv, w_out, w_in, w_down)
        )
        out_x, out_y = call(pick_kernel, edges, (tokens, send_x, send_y), "pick")
        filled = jnp.broadcast_to(lengths[:, None], context.shape)
    else:
        qkv, out, into, down = w_qkv, w_out, w_in, w_down
        size = qkv.shape[0] // 4
        share_qkv = Share(0, "gx", size, size)
        share_out = Share(0, "core", out.shape[0] // 2, out.shape[0] // 2)
        share_in = Share(0, "gy", into.shape[0] // 4, into.shape[0] // 4)
        size = down.shape[0] // 8
        share_early = Share(0, "gx", size, size)
        share_late = Share(4 * size, "core", 2 * size, 2 * size)
        tokens, gain_one, gain_two, context, filled, out_x, out_y, part_qkv = call(
            lambda *refs: prepare_kernel([share_qkv], *refs),
            [
                struct(rows, width), struct(1, width, jnp.float32), struct(1, width, jnp.float32),
                struct(*context.shape, jnp.int32), struct(*context.shape, jnp.int32),
            ]
            + edges + [struct(share_qkv.rows, width)],
            (tokens, gain_one, gain_two, send_x, send_y, context, lengths, qkv), "prepare",
            [
                pltpu.VMEM(send_x.shape, jnp.int32), pltpu.VMEM(send_y.shape, jnp.int32),
                pltpu.SMEM(lengths.shape, jnp.int32), pltpu.SemaphoreType.DMA((8,)),
            ],
            [HBM] * 8,
        )
        y_qkv = swap(part_qkv, "fsdp", 1)
        groups = [[share_in], [share_out, share_early], [share_late]]
        later, out_x = after(((w_in, w_out, w_down), out_x))
        parts = call(
            lambda *refs: slice_kernel(groups, *refs),
            [struct(sum(share.rows for share in group), width) for group in groups],
            (*later, later[2]), "slices", [pltpu.SemaphoreType.DMA((4,))], [HBM] * 4,
        )
        y_in, y_middle, y_late = (swap(part, "fsdp", 1) for part in parts)

    def crossed(share, near, flip=0):
        return [(share, flip, near), (share, flip + 1, swap(near, "gx", 1))]

    def arrays(pieces):
        return [piece[2] for piece in pieces]

    def plan(pieces):
        return [piece[:2] for piece in pieces]

    halo_x = ring(out_x, "gx")
    halo_y = ring(out_y, "gy")
    if paired:
        normed, chosen, *projected, into, down = call(
            context_kernel, [struct(rows, width)] * 7 + [struct(*into.shape), struct(*down.shape)],
            (tokens, halo_x, halo_y, gain_one, context, qkv, into, down), "context",
            [pltpu.VMEM(qkv.shape, jnp.bfloat16), pltpu.SemaphoreType.DMA((3,))], [VMEM] * 5 + [HBM] * 3,
        )
    else:
        normed, chosen = call(
            context_rows, [struct(rows, width)] * 2, (tokens, halo_x, halo_y, gain_one, context), "context"
        )
    if paired:
        x_qkv = swap(y_qkv, "gx", 2)
        x_qkv, y_in, chosen = after((x_qkv, y_in, chosen))
        z_in = swap(y_in, "gy", 1)
        if 1:
            chosen, y_in = after((chosen, y_in))
    if paired:
        pieces = crossed(share_qkv, y_qkv) + [(share_qkv, 2, x_qkv)]
        size = share_qkv.rows // 1
        for low in range(0, share_qkv.rows, size):
            pieces.append((share_qkv._replace(base=low, rows=size), 3, swap(x_qkv[low : low + size], "gx", 1)))
        count = 2 + len(pieces)
        projected = call(
            lambda *refs, plan=plan(pieces): project_rest_kernel(plan, *refs), [struct(rows, width)] * 5,
            (normed, chosen, *arrays(pieces), *projected), "project", [pltpu.VMEM(qkv.shape, jnp.bfloat16)],
            aliases={count + number: number for number in range(5)},
        )
    else:
        projected = call(project_kernel, [struct(rows, width)] * 5, (normed, chosen, qkv), "project")

    def attend(windows):
        return call(
            lambda *refs: attend_kernel(windows, *refs), [struct(len(windows) * WIN, width)],
            (filled, *projected), "attend",
        )

    windows = list(range(rows // WIN))
    half = len(windows) // 2
    mixed = attend(windows[:half])
    pieces_out, pieces_in, pieces_down, pieces_last = [], [], [], []
    if 0:
        mixed += attend(windows[half:])
    if paired:
        y_middle, mixed = after((y_middle, mixed))
        y_out, y_early = y_middle[: share_out.rows], y_middle[share_out.rows :]
        x_early = swap(y_early, "gx", 2)
        projected, y_out, y_early = after((projected, y_out, y_early))
    if not 0:
        mixed += attend(windows[half:])
    if paired:
        pieces_out = crossed(share_out, y_out)
        if 1 == 0:
            z_in, mixed = after((z_in, mixed))
    middle, second = call(
        lambda *refs: finish_kernel(len(mixed), plan(pieces_out), *refs),
        [struct(rows, width, jnp.float32), struct(rows, width)], (tokens, gain_two, out, *mixed, *arrays(pieces_out)),
        "finish", [pltpu.VMEM((width, width), jnp.bfloat16)],
    )

    if paired and 1:
        z_in, second = after((z_in, second))
        pieces = crossed(share_in, y_in) + crossed(share_in, z_in, 2)
        z_in, second = after((z_in, second))
    (total,) = call(
        feed_kernel, [struct(rows, width, jnp.float32 if paired else jnp.bfloat16)], (middle, second, into, down), "feed"
    )
    if not paired:
        return total
    if 1 == 0:
        pieces = crossed(share_in, y_in) + crossed(share_in, z_in, 2)
    if 0:
        y_late, total = after((y_late, total))
    else:
        x_early, y_late, total = after((x_early, y_late, total))
    late = swap(y_late, "gx", 1)
    here = [(share_early, 0, y_early), (share_late, 0, y_late)]
    hidden, total = call(
        lambda *refs, plan=plan(pieces): hidden_kernel(plan, [piece[:2] for piece in here], *refs),
        [struct(rows, into.shape[0]), struct(rows, width, jnp.float32)],
        (total, second, *arrays(pieces), *arrays(here)), "hidden",
    )
    if 0:
        x_early, hidden = after((x_early, hidden))
    rest = [(share_early, 1, swap(y_early, "gx", 1))] + crossed(share_early, x_early, 2) + [(share_late, 1, late)]
    return call(
        lambda *refs: last_kernel(plan(rest), *refs), [struct(rows, width)],
        (total, hidden, *arrays(rest)), "last",
        [pltpu.VMEM((rows, width), jnp.bfloat16), pltpu.SemaphoreType.DMA((4,))], result=HBM,
    )[0]


def solution(mesh):
    in_specs = (
        P(("gx", "gy", "fsdp"), None),
        P(),
        P(),
        P("fsdp", None),
        P("fsdp", None),
        P("fsdp", None),
        P("fsdp", None),
        P(("gx", "gy", "fsdp")),
        P(("gx", "gy", "fsdp")),
        P(("gx", "gy", "fsdp"), None),
        P(("gx", "gy", "fsdp")),
    )
    out_specs = P(("gx", "gy", "fsdp"), None)
    return jax.shard_map(body, mesh=mesh, in_specs=in_specs, out_specs=out_specs, check_vma=False)
```
